256 devices in a mesh: strip: 8 (over z), along: 32 (over y, x, core).
Axes of the slice: x: 4, y: 4, z: 8, core: 2. Of those that a mesh axis runs over, the one named last changes fastest.
Arguments:
- heights: float32 [4096, 16384], P('strip', 'along'), may hold values from -6 to 6
- confidence: float32 [4096, 16384], P('strip', 'along'), may hold values from 0.25 to 4
- survey_ids: int32 [4096, 16384], P('strip', 'along'), may hold values from 0 to 39
- seam_mask: int32 [4096, 16384], P('strip', 'along'), may hold values 0 or 1
- datum: float32 [40], replicated, may hold values from -4 to 4
Outputs:
- merged: float32 [4096, 16384], P('strip', 'along')
- offsets: float32 [40, 4096], P(None, 'strip')
The draws below stay inside these ranges and needn't reach their ends.
All inputs are finite; a program needn't handle non-finite values. No bound on the sum of `seam_mask` on one device may be relied on, other than what follows from the above.
Results may differ from the reference program's by a relative error of at most 0.0003.
Values sent between devices are 32-bit elements; how exact they have to be, the bound alone decides.
A program may use at most 64 MiB of HBM per device.

```python
import math
import jax
import jax.numpy as jnp
import numpy as np
from jax import lax

SURVEYS = 40
SWEEPS = 4
NR = 4096
NC = 16384


def set_ends(values, rng, low, largest):
    longest = values.shape.index(max(values.shape))
    spots = []
    for shift in (0, 1):
        where = [jax.random.randint(jax.random.fold_in(rng, axis), (), 0, length) for axis, length in enumerate(values.shape)]
        where[longest] = (where[longest] + shift) % values.shape[longest]
        spots.append(tuple(where))
    return values.at[spots[0]].set(low).at[spots[1]].set(largest)


def level_of(key, extent, pieces, least, top_value):
    level, own = 1.0, jax.random.fold_in(key, 6)
    for position, shards_of in pieces:
        steps = jnp.exp(jax.random.uniform(jax.random.fold_in(own, position), (shards_of,), jnp.float32, least / len(pieces), top_value / len(pieces)))
        level = level * jnp.repeat(steps, extent[position] // shards_of).reshape([-1 if axis == position else 1 for axis in range(len(extent))])
    return level


def rank_bounds(amount, lean):
    weights = [(1 << 20) // math.isqrt(rank ** lean) + 1 for rank in range(1, amount + 1)]
    scale = 1 + sum(weights) // (1 << 30)
    return np.cumsum(np.array([max(1, weight // scale) for weight in weights]))


def ranked(stream_key, dims, number_of, skew):
    grid = rank_bounds(number_of, skew)
    lot = jax.random.randint(jax.random.fold_in(stream_key, 1), dims, 0, int(grid[number_of - 1]))
    grade = jnp.searchsorted(jnp.asarray(grid, jnp.int32), lot, side="right")
    return jax.random.permutation(jax.random.fold_in(stream_key, 2), number_of)[grade].astype(jnp.int32)


def noise(own_key, shape, deviation, limit, cuts=(), kind=jnp.bfloat16):
    entries = deviation * jax.random.normal(own_key, shape, jnp.float32)
    if cuts:
        entries = entries * level_of(own_key, shape, cuts, -0.22, 0.18)
    return jnp.clip(entries, -limit, limit).astype(kind)


def setup_inputs(seed: int = 0) -> dict:
    keys = jax.random.split(jax.random.key(seed), 6)
    heights = noise(keys[0], (NR, NC), 1.0, 6.0, ((0, 8), (1, 32)), jnp.float32)
    confidence = jnp.clip(jnp.exp(math.log(4.0) - 2.7725887 * jax.random.uniform(keys[1], (NR, NC), jnp.float32) ** level_of(keys[1], (NR, NC), ((0, 8), (1, 32)), -0.2, 0.2)), 0.25, 4.0)
    survey_ids = set_ends(ranked(keys[2], (NR, NC), SURVEYS, 2), jax.random.fold_in(keys[2], 3), 0, SURVEYS - 1).astype(jnp.int32)
    seam_mask = set_ends((jax.random.randint(keys[3], (NR, NC), 0, 64) < 1).astype(jnp.int32), jax.random.fold_in(keys[3], 1), 0, 1)
    datum = noise(keys[4], (SURVEYS,), 1.0, 4.0, (), jnp.float32)
    return {"heights": heights, "confidence": confidence, "survey_ids": survey_ids, "seam_mask": seam_mask, "datum": datum}


smooth_weight = 1.0
centre_value = 1.05
half_width = 0.95


def neighbour_sum(values):
    padded = jnp.pad(values, 1)
    return padded[2:, 1:-1] + padded[:-2, 1:-1] + padded[1:-1, 2:] + padded[1:-1, :-2]


def survey_profile(survey_ids, values):
    row_count, col_count = survey_ids.shape
    block_rows = min(128, row_count)
    block_count = row_count // block_rows
    labels = jnp.arange(SURVEYS, dtype=jnp.int32)[:, None, None]

    def per_block(block):
        ids_block, value_block = block
        matches = ids_block[None] == labels
        return jnp.sum(jnp.where(matches, value_block[None], 0.0), axis=2)

    sums = lax.map(per_block, (survey_ids.reshape(block_count, block_rows, col_count), values.reshape(block_count, block_rows, col_count)))
    return sums.transpose(1, 0, 2).reshape(SURVEYS, row_count)


def spread_table(survey_ids, lookup_table):
    row_count, col_count = survey_ids.shape
    block_rows = min(128, row_count)
    block_count = row_count // block_rows
    labels = jnp.arange(SURVEYS, dtype=jnp.int32)[:, None, None]
    blocks = lookup_table.reshape(SURVEYS, block_count, block_rows).transpose(1, 0, 2)

    def per_block(block):
        ids_block, table_block = block
        matches = ids_block[None] == labels
        return jnp.sum(jnp.where(matches, table_block[:, :, None], 0.0), axis=0)

    spread = lax.map(per_block, (survey_ids.reshape(block_count, block_rows, col_count), blocks))
    return spread.reshape(row_count, col_count)


def reference(heights, confidence, survey_ids, seam_mask, datum):
    row_count = heights.shape[0]
    datum_rows = jnp.broadcast_to(datum[:, None], (SURVEYS, row_count))
    observed = heights + spread_table(survey_ids, datum_rows)
    merged = observed
    diagonal = confidence + 4.0 * smooth_weight
    seam_weight = seam_mask.astype(jnp.float32) * confidence
    profile_weight = survey_profile(survey_ids, seam_weight)
    sigma_value = centre_value / half_width
    ratio_now = 1.0 / sigma_value
    direction = jnp.zeros_like(merged)
    offsets = jnp.zeros((SURVEYS, row_count), jnp.float32)
    for sweep_index in range(SWEEPS):
        beside = neighbour_sum(merged)
        gap = seam_weight * (0.25 * beside - observed)
        profile_gap = survey_profile(survey_ids, gap)
        level = jnp.sum(gap) / (jnp.sum(seam_weight) + 1.0)
        offsets = profile_gap / jnp.maximum(profile_weight, 1.0) - level
        target = observed + spread_table(survey_ids, offsets)
        residual = confidence * (target - merged) - smooth_weight * (4.0 * merged - beside)
        scaled = residual / diagonal
        if sweep_index == 0:
            direction = scaled / centre_value
        else:
            ratio_next = 1.0 / (2.0 * sigma_value - ratio_now)
            direction = ratio_next * ratio_now * direction + (2.0 * ratio_next / half_width) * scaled
            ratio_now = ratio_next
        merged = merged + direction
    return merged, offsets
```

```python
import functools

import jax
import jax.numpy as jnp
from jax import lax
from jax.experimental import pallas as pl
from jax.experimental.pallas import tpu as pltpu
from jax.sharding import PartitionSpec as P

SURVEYS = 40
SWEEPS = 4

smooth_weight = 1.0
centre_value = 1.05
half_width = 0.95

LANES = 128
DEPTH = 4
MESH = pl.DeviceIdType.MESH
F32 = jnp.float32
BF16 = jnp.bfloat16
I32 = jnp.int32


def coefficients():
    sigma_value = centre_value / half_width
    ratio_now = 1.0 / sigma_value
    pairs = [(0.0, 1.0 / centre_value)]
    for _ in range(SWEEPS - 1):
        ratio_next = 1.0 / (2.0 * sigma_value - ratio_now)
        pairs.append((ratio_next * ratio_now, 2.0 * ratio_next / half_width))
        ratio_now = ratio_next
    return pairs


def torus_distance(step, size):
    return min(step % size, (-step) % size)


def lane_take(values, index):
    return jnp.take_along_axis(values, index, axis=1, mode="promise_in_bounds")


def lanes_of(rows):
    return lax.broadcasted_iota(I32, (rows, LANES), 1)


def kernel(
    zsize,
    dims,
    heights,
    confidence,
    survey_ids,
    seam_mask,
    datum,
    merged_out,
    offsets_out,
    mm,
    ids,
    obs,
    q,
    cq,
    pp,
    w,
    d,
    bes,
    mask,
    onehot,
    dat,
    strip_send,
    strip_recv,
    hist,
    parts,
    floor,
    zsend,
    zrecv,
    table,
    wtotal,
    offs,
    load_sem,
    store_sem,
    strip_ss,
    strip_rs,
    row_ss,
    row_rs,
    part_ss,
    part_rs,
    z_ss,
    z_rs,
    table_ss,
    table_rs,
):
    ny, nx, nc = dims
    along = ny * nx * nc
    rows, cols = heights.shape
    tiles = cols // LANES
    groups = rows // 32
    zi = lax.axis_index("strip")
    me = lax.axis_index("along")
    my_y, my_x, my_c = me // (nx * nc), (me // nc) % nx, me % nc

    steps = [(a, b, c) for a in range(ny) for b in range(nx) for c in range(nc)]
    steps = sorted(steps[1:], key=lambda s: -(torus_distance(s[0], ny) + torus_distance(s[1], nx) + 0.3 * s[2]))

    def partner(step):
        a, b, c = step
        return (((my_y + a) % ny) * nx + (my_x + b) % nx) * nc + (my_c + c) % nc

    def slot_of(step):
        a, b, c = step
        return (((-a) % ny) * nx + (-b) % nx) * nc + (-c) % nc

    loads = []
    for t in range(tiles):
        for n, (src, dst) in enumerate(((survey_ids, ids), (confidence, cq), (heights, obs), (seam_mask, mask))):
            copy = pltpu.make_async_copy(src.at[:, pl.ds(t * LANES, LANES)], dst.at[t], load_sem.at[n, t])
            copy.start()
            loads.append((n, copy))

    mm[:, 0:8, :] = jnp.zeros((tiles + 1, 8, LANES), F32)
    mm[:, rows + 8 : rows + 16, :] = jnp.zeros((tiles + 1, 8, LANES), F32)
    strip_recv[...] = jnp.zeros(strip_recv.shape, F32)

    barrier = pltpu.get_barrier_semaphore()
    for step in steps:
        pl.semaphore_signal(barrier, inc=1, device_id=(zi, partner(step)), device_id_type=MESH)
    for k in range(1, zsize):
        pl.semaphore_signal(barrier, inc=1, device_id=((zi + k) % zsize, me), device_id_type=MESH)

    dat[...] = jnp.zeros((16, LANES), F32)
    dat[:, 0:SURVEYS] = jnp.broadcast_to(datum[...], (16, SURVEYS))

    for n, copy in loads:
        if n < 3:
            copy.wait()

    def pack_strip(b, _):
        r = pl.ds(pl.multiple_of(b * 32, 32), 32)
        lane = lanes_of(32)
        first, last = 0, tiles - 1
        low = jnp.where(lane < 4, ids[first, r, :].astype(F32), pltpu.roll(cq[first, r, :], 4, 1))
        low = jnp.where(lane < 8, low, pltpu.roll(obs[first, r, :], 8, 1))
        high = jnp.where(lane >= 124, ids[last, r, :].astype(F32), pltpu.roll(cq[last, r, :], LANES - 4, 1))
        high = jnp.where(lane >= 120, high, pltpu.roll(obs[last, r, :], LANES - 8, 1))
        bes[0, r, :] = jnp.where(lane < 64, low, high)
        return 0

    lax.fori_loop(0, rows // 32, pack_strip, 0)
    span = min(rows, LANES)
    for b in range(rows // span):
        strip_send[b] = bes[0, b * span : (b + 1) * span, :].T

    pl.semaphore_wait(barrier, along + zsize - 2)

    def strip_copy(side):
        at = pl.ds(0, 16) if side == 0 else pl.ds(112, 16)
        return pltpu.make_async_remote_copy(
            strip_send.at[:, at, :],
            strip_recv.at[:, at, :],
            strip_ss.at[side],
            strip_rs.at[side],
            device_id=(zi, me - 1 if side == 0 else me + 1),
            device_id_type=MESH,
        )

    has = (me > 0, me < along - 1)
    for side in range(2):

        @pl.when(has[side])
        def _():
            strip_copy(side).start()

    def make_onehot(g, _):
        sub = lax.broadcasted_iota(I32, (8, LANES), 0)
        for t in range(tiles):
            block = ids[t, pl.ds(pl.multiple_of(g * 32, 32), 32), :] & 7
            for r in range(0, 32, 2):
                pair = [
                    jnp.where(jnp.broadcast_to(block[r + i : r + i + 1, :], (8, LANES)) == sub, 1.0, 0.0)
                    for i in range(2)
                ]
                onehot[g, r * 8 : r * 8 + 16, t * LANES : (t + 1) * LANES] = jnp.concatenate(pair, 0).astype(BF16)
        return 0

    lax.fori_loop(0, groups, make_onehot, 0)

    def profile(values, hid, g):
        high = values.astype(BF16)
        low = (values - high.astype(F32)).astype(BF16)
        zero = jnp.zeros_like(high)
        match = [hid == h for h in range(5)]
        left = jnp.concatenate([jnp.where(m, p, zero) for p in (high, low) for m in match], 0)
        full = lax.dot_general(left, onehot[g], (((1,), (1,)), ((), ())), preferred_element_type=F32)
        full = full[:160] + full[160:]
        own = lax.broadcasted_iota(I32, (32, 256), 0) == lax.broadcasted_iota(I32, (32, 256), 1) // 8
        sums = [jnp.sum(jnp.where(own, full[32 * h : 32 * h + 32], 0.0), axis=0, keepdims=True) for h in range(5)]
        return jnp.concatenate(sums + [jnp.zeros((3, 256), F32)], 0)

    def high_bits(r):
        return jnp.concatenate([(ids[t, r, :] >> 3) & 7 for t in range(tiles)], 1)

    def put_profile(n, g, sums):
        hist[n, 2 * g] = sums[:, :LANES]
        hist[n, 2 * g + 1] = sums[:, LANES:]

    def part_copy(n, step):
        to = partner(step)
        return pltpu.make_async_remote_copy(
            hist.at[n, to],
            parts.at[n, slot_of(step)],
            part_ss.at[n],
            part_rs.at[n],
            device_id=(zi, to),
            device_id_type=MESH,
        )

    def all_parts(n):
        return pltpu.make_async_remote_copy(
            hist.at[n, pl.ds(1, along - 1)],
            parts.at[n, pl.ds(1, along - 1)],
            part_ss.at[n],
            part_rs.at[n],
            device_id=(zi, me),
            device_id_type=MESH,
        )

    def z_copy(n, k):
        return pltpu.make_async_remote_copy(
            zsend.at[n],
            zrecv.at[n, zsize - k],
            z_ss.at[n],
            z_rs.at[n],
            device_id=((zi + k) % zsize, me),
            device_id_type=MESH,
        )

    def all_z(n):
        return pltpu.make_async_remote_copy(
            zrecv.at[n, pl.ds(1, zsize - 1)],
            zrecv.at[n, pl.ds(1, zsize - 1)],
            z_ss.at[n],
            z_rs.at[n],
            device_id=(zi, me),
            device_id_type=MESH,
        )

    def send_profile(n):
        total = jnp.sum(hist[n], axis=0)
        zsend[n] = total
        zrecv[n, 0] = total
        for k in sorted(range(1, zsize), key=lambda k: -torus_distance(k, zsize)):
            z_copy(n, k).start()
        for step in steps:
            part_copy(n, step).start()
        parts[n, 0] = hist[n, me]

    def summed_parts(n):
        all_parts(n).wait_recv()
        return jnp.sum(parts[n], axis=0)

    def summed_z(n):
        all_z(n).wait_recv()
        return jnp.broadcast_to(jnp.sum(jnp.sum(zrecv[n], axis=0), keepdims=True), (8, LANES))

    for n, copy in loads:
        if n == 3:
            copy.wait()

    def weights(g, _):
        r = pl.ds(pl.multiple_of(g * 32, 32), 32)
        values = []
        for t in range(tiles):
            value = mask[t, r, :].astype(F32) * cq[t, r, :]
            w[t, r, :] = value
            values.append(value)
        put_profile(SWEEPS, g, profile(jnp.concatenate(values, 1), high_bits(r), g))
        return 0

    lax.fori_loop(0, groups, weights, 0)
    send_profile(SWEEPS)

    for side in range(2):

        @pl.when(has[1 - side])
        def _():
            strip_copy(side).wait_recv()

    for b in range(rows // span):
        bes[0, b * span : (b + 1) * span, :] = strip_recv[b].T

    def prepare(b, _):
        r = pl.ds(pl.multiple_of(b * 16, 16), 16)
        lane = lanes_of(16)
        upper = jnp.where(lax.broadcasted_iota(I32, (16, LANES), 0) >= 8, 64, 0)
        got = bes[0, r, :]
        edge_low, edge_high = lane < DEPTH, lane >= LANES - DEPTH
        ids[tiles, r, :] = jnp.where(edge_low | edge_high, got, 0.0).astype(I32)
        cq[tiles, r, :] = jnp.where(
            edge_low, pltpu.roll(got, LANES - 4, 1), jnp.where(edge_high, pltpu.roll(got, 4, 1), 0.0)
        )
        obs[tiles, r, :] = jnp.where(
            edge_low, pltpu.roll(got, LANES - 8, 1), jnp.where(edge_high, pltpu.roll(got, 8, 1), 0.0)
        )
        for t in range(tiles + 1):
            survey = ids[t, r, :]
            weight = cq[t, r, :]
            seen = obs[t, r, :] + lane_take(dat[...], survey)
            inverse = 1.0 / (weight + 4.0 * smooth_weight)
            if t == tiles:
                inside = weight > 0.0
                seen = jnp.where(inside, seen, 0.0)
                inverse = jnp.where(inside, inverse, 0.0)
            share = weight * inverse
            ids[t, r, :] = survey + upper
            obs[t, r, :] = seen
            q[t, r, :] = inverse
            cq[t, r, :] = share
            pp[t, r, :] = share * seen
            mm[t, pl.ds(pl.multiple_of(b * 16 + 8, 8), 16), :] = seen
        return 0

    lax.fori_loop(0, rows // 16, prepare, 0)

    def row_copy(k, side):
        at, to = ((8, rows + 8), (rows + 7, 7))[side]
        return pltpu.make_async_remote_copy(
            mm.at[:, pl.ds(at, 1), :],
            mm.at[:, pl.ds(to, 1), :],
            row_ss.at[k, side],
            row_rs.at[k, side],
            device_id=(zi - 1 if side == 0 else zi + 1, me),
            device_id_type=MESH,
        )

    above = (zi > 0, zi < zsize - 1)

    def send_rows(k):
        for side in range(2):

            @pl.when(above[side])
            def _():
                row_copy(k, side).start()

    def wait_rows(k):
        for side in range(2):

            @pl.when(above[1 - side])
            def _():
                row_copy(k, side).wait_recv()

        for side in range(2):

            @pl.when(above[side])
            def _():
                row_copy(k, side).wait_send()

    send_rows(0)

    def stencil_group(k, g):
        first = g * 32
        r = pl.ds(pl.multiple_of(first, 32), 32)
        lane = lanes_of(32)
        now = [mm[t, pl.ds(pl.multiple_of(first + 8, 8), 32), :] for t in range(tiles + 1)]
        gaps = []
        for t in range(tiles + 1):
            before, after = now[(t - 1) % (tiles + 1)], now[(t + 1) % (tiles + 1)]
            value = mm[t, pl.ds(first + 7, 32), :] + mm[t, pl.ds(first + 9, 32), :]
            value += pltpu.roll(jnp.where(lane == LANES - 1, before, now[t]), 1, 1)
            value += pltpu.roll(jnp.where(lane == 0, after, now[t]), LANES - 1, 1)
            bes[t, r, :] = value
            if t < tiles:
                gaps.append(w[t, r, :] * (0.25 * value - obs[t, r, :]))
        put_profile(k, g, profile(jnp.concatenate(gaps, 1), high_bits(r), g))

    def local_update(k, alpha, beta):
        def block(b, _):
            r = pl.ds(pl.multiple_of(b * 32, 32), 32)
            for t in range(tiles + 1):
                now = mm[t, pl.ds(pl.multiple_of(b * 32 + 8, 8), 32), :]
                value = beta * (pp[t, r, :] + q[t, r, :] * bes[t, r, :] - now)
                if k > 0:
                    value += alpha * d[t, r, :]
                d[t, r, :] = value
            return 0

        lax.fori_loop(0, rows // 32, block, 0)

    def owner_tile(k):
        sums = summed_parts(k)
        if k == 0:
            floor[...] = jnp.maximum(summed_parts(SWEEPS), 1.0)
        share = sums / floor[...]
        lane = lanes_of(8)
        sub = lax.broadcasted_iota(I32, (8, LANES), 0)
        index = 8 * (sub + jnp.where(lane >= 64, 8, 0)) + (lane & 7)
        kind = (lane & 63) >> 3
        tile = jnp.zeros((8, LANES), F32)
        for h in range(5):
            tile = jnp.where(kind == h, lane_take(jnp.broadcast_to(share[h : h + 1], (8, LANES)), index), tile)
        tile = jnp.where(kind == 5, summed_z(k), tile)
        if k == 0:
            tile = jnp.where(kind > 5, summed_z(SWEEPS), tile)
        table[k, me] = tile

    def table_copy(k, step):
        return pltpu.make_async_remote_copy(
            table.at[k, me],
            table.at[k, me],
            table_ss.at[k],
            table_rs.at[k],
            device_id=(zi, partner(step)),
            device_id_type=MESH,
        )

    def all_table(k):
        return pltpu.make_async_remote_copy(
            table.at[k, pl.ds(0, along - 1)],
            table.at[k, pl.ds(0, along - 1)],
            table_ss.at[k],
            table_rs.at[k],
            device_id=(zi, me),
            device_id_type=MESH,
        )

    stores = []
    for k, (alpha, beta) in enumerate(coefficients()):
        last = k == SWEEPS - 1

        def inner(g, _, k=k):
            stencil_group(k, g)
            return 0

        lax.fori_loop(1, groups - 1, inner, 0)
        wait_rows(k)
        stencil_group(k, 0)
        stencil_group(k, groups - 1)
        send_profile(k)
        local_update(k, alpha, beta)

        owner_tile(k)
        for step in steps:
            table_copy(k, step).start()
        all_table(k).wait_recv()

        whole = jnp.sum(table[k], axis=0)
        if k == 0:
            wtotal[...] = lane_take(whole, jnp.full((8, LANES), 48, I32)) + 1.0
        level = lane_take(whole, jnp.full((8, LANES), 40, I32)) / wtotal[...]
        level = jnp.concatenate([level, level], 0)

        def update(b, _, k=k, last=last, beta=beta, level=level):
            r = pl.ds(pl.multiple_of(b * 16, 16), 16)
            at = pl.ds(pl.multiple_of(b * 16 + 8, 8), 16)
            row_table = table[k, b]
            row_table = jnp.concatenate([row_table, row_table], 0) - level
            for t in range(tiles if last else tiles + 1):
                step = d[t, r, :] + beta * cq[t, r, :] * lane_take(row_table, ids[t, r, :])
                if not last:
                    d[t, r, :] = step
                mm[t, at, :] = mm[t, at, :] + step
            return 0

        if not last:
            update(0, 0)
            update(rows // 16 - 1, 0)
            send_rows(k + 1)
            lax.fori_loop(1, rows // 16 - 1, update, 0)
        else:
            chunks = 4
            for c in range(chunks):
                size = rows // chunks
                lax.fori_loop(c * size // 16, (c + 1) * size // 16, update, 0)
                for t in range(tiles):
                    copy = pltpu.make_async_copy(
                        mm.at[t, pl.ds(8 + c * size, size), :],
                        merged_out.at[pl.ds(c * size, size), pl.ds(t * LANES, LANES)],
                        store_sem.at[c, t],
                    )
                    copy.start()
                    stores.append(copy)
            for b in range(rows // span):
                pieces = []
                for o in range(b * span // 16, (b + 1) * span // 16):
                    piece = table[k, o] - level[:8]
                    pieces += [piece, pltpu.roll(piece, 64, 1)]
                offs[:, b * span : (b + 1) * span] = jnp.concatenate(pieces, 0).T[:SURVEYS]
            copy = pltpu.make_async_copy(offs, offsets_out, store_sem.at[chunks, 0])
            copy.start()
            stores.append(copy)

    for side in range(2):

        @pl.when(has[side])
        def _():
            strip_copy(side).wait_send()

    for n in range(SWEEPS + 1):
        all_parts(n).wait_send()
        all_z(n).wait_send()
    for k in range(SWEEPS):
        all_table(k).wait_send()
    for copy in stores:
        copy.wait()


def solution(mesh):
    zsize, along = mesh.shape["strip"], mesh.shape["along"]
    dims = (4, 4, 2) if along == 32 else (1, along // 2, 2)

    def on_device(heights, confidence, survey_ids, seam_mask, datum):
        rows, cols = heights.shape
        assert rows == 16 * along and cols % 256 == 0
        tiles = cols // LANES
        wide = (tiles + 1, rows, LANES)
        narrow = (tiles, rows, LANES)
        span = min(rows, LANES)
        strip = (rows // span, LANES, span)
        dma = pltpu.SemaphoreType.DMA
        scratch = [
            pltpu.VMEM((tiles + 1, rows + 16, LANES), F32),
            pltpu.VMEM(wide, I32),
            pltpu.VMEM(wide, F32),
            pltpu.VMEM(wide, F32),
            pltpu.VMEM(wide, F32),
            pltpu.VMEM(wide, F32),
            pltpu.VMEM(narrow, F32),
            pltpu.VMEM(wide, F32),
            pltpu.VMEM(wide, F32),
            pltpu.VMEM(narrow, I32),
            pltpu.VMEM((rows // 32, 256, cols), BF16),
            pltpu.VMEM((16, LANES), F32),
            pltpu.VMEM(strip, F32),
            pltpu.VMEM(strip, F32),
            pltpu.VMEM((SWEEPS + 1, along, 8, LANES), F32),
            pltpu.VMEM((SWEEPS + 1, along, 8, LANES), F32),
            pltpu.VMEM((8, LANES), F32),
            pltpu.VMEM((SWEEPS + 1, 8, LANES), F32),
            pltpu.VMEM((SWEEPS + 1, zsize, 8, LANES), F32),
            pltpu.VMEM((SWEEPS, along, 8, LANES), F32),
            pltpu.VMEM((8, LANES), F32),
            pltpu.VMEM((SURVEYS, rows), F32),
            dma((4, tiles)),
            dma((5, tiles)),
            dma((2,)),
            dma((2,)),
            dma((SWEEPS, 2)),
            dma((SWEEPS, 2)),
            dma((SWEEPS + 1,)),
            dma((SWEEPS + 1,)),
            dma((SWEEPS + 1,)),
            dma((SWEEPS + 1,)),
            dma((SWEEPS,)),
            dma((SWEEPS,)),
        ]
        return pl.pallas_call(
            functools.partial(kernel, zsize, dims),
            out_shape=(
                jax.ShapeDtypeStruct((rows, cols), F32),
                jax.ShapeDtypeStruct((SURVEYS, rows), F32),
            ),
            in_specs=[pl.BlockSpec(memory_space=pl.ANY)] * 4 + [pl.BlockSpec(memory_space=pltpu.VMEM)],
            out_specs=(pl.BlockSpec(memory_space=pl.ANY), pl.BlockSpec(memory_space=pl.ANY)),
            scratch_shapes=scratch,
            compiler_params=pltpu.CompilerParams(
                collective_id=0, has_side_effects=True, vmem_limit_bytes=44 * 1024 * 1024
            ),
        )(heights, confidence, survey_ids, seam_mask, datum.reshape(1, SURVEYS))

    return jax.shard_map(
        on_device,
        mesh=mesh,
        in_specs=(P("strip", "along"),) * 4 + (P(),),
        out_specs=(P("strip", "along"), P(None, "strip")),
        check_vma=False,
    )
```

```python
import functools

import jax
import jax.numpy as jnp
from jax import lax
from jax.experimental import pallas as pl
from jax.experimental.pallas import tpu as pltpu
from jax.sharding import PartitionSpec as P

SURVEYS = 40
SWEEPS = 4

smooth_weight = 1.0
centre_value = 1.05
half_width = 0.95

LANES = 128
DEPTH = 4
MESH = pl.DeviceIdType.MESH
F32 = jnp.float32
BF16 = jnp.bfloat16
I32 = jnp.int32


def coefficients():
    sigma_value = centre_value / half_width
    ratio_now = 1.0 / sigma_value
    pairs = [(0.0, 1.0 / centre_value)]
    for _ in range(SWEEPS - 1):
        ratio_next = 1.0 / (2.0 * sigma_value - ratio_now)
        pairs.append((ratio_next * ratio_now, 2.0 * ratio_next / half_width))
        ratio_now = ratio_next
    return pairs


def torus_distance(step, size):
    return min(step % size, (-step) % size)


def lane_take(values, index):
    return jnp.take_along_axis(values, index, axis=1, mode="promise_in_bounds")


def lanes_of(rows):
    return lax.broadcasted_iota(I32, (rows, LANES), 1)


def kernel(
    zsize,
    dims,
    heights,
    confidence,
    survey_ids,
    seam_mask,
    datum,
    merged_out,
    offsets_out,
    mm,
    ids,
    obs,
    q,
    cq,
    pp,
    w,
    d,
    bes,
    mask,
    onehot,
    dat,
    strip_send,
    strip_recv,
    hist,
    parts,
    floor,
    zsend,
    zrecv,
    table,
    wtotal,
    offs,
    load_sem,
    store_sem,
    strip_ss,
    strip_rs,
    row_ss,
    row_rs,
    part_ss,
    part_rs,
    z_ss,
    z_rs,
    table_ss,
    table_rs,
):
    ny, nx, nc = dims
    along = ny * nx * nc
    rows, cols = heights.shape
    tiles = cols // LANES
    groups = rows // 32
    zi = lax.axis_index("strip")
    me = lax.axis_index("along")
    my_y, my_x, my_c = me // (nx * nc), (me // nc) % nx, me % nc

    steps = [(a, b, c) for a in range(ny) for b in range(nx) for c in range(nc)]
    steps = sorted(steps[1:], key=lambda s: -(torus_distance(s[0], ny) + torus_distance(s[1], nx) + 0.3 * s[2]))

    def partner(step):
        a, b, c = step
        return (((my_y + a) % ny) * nx + (my_x + b) % nx) * nc + (my_c + c) % nc

    def slot_of(step):
        a, b, c = step
        return (((-a) % ny) * nx + (-b) % nx) * nc + (-c) % nc

    loads = []
    for t in range(tiles):
        for n, (src, dst) in enumerate(((survey_ids, ids), (confidence, cq), (heights, obs), (seam_mask, mask))):
            copy = pltpu.make_async_copy(src.at[:, pl.ds(t * LANES, LANES)], dst.at[t], load_sem.at[n, t])
            copy.start()
            loads.append((n, copy))

    mm[:, 0:8, :] = jnp.zeros((tiles + 1, 8, LANES), F32)
    mm[:, rows + 8 : rows + 16, :] = jnp.zeros((tiles + 1, 8, LANES), F32)
    strip_recv[...] = jnp.zeros(strip_recv.shape, F32)

    barrier = pltpu.get_barrier_semaphore()
    for step in steps:
        pl.semaphore_signal(barrier, inc=1, device_id=(zi, partner(step)), device_id_type=MESH)
    for k in range(1, zsize):
        pl.semaphore_signal(barrier, inc=1, device_id=((zi + k) % zsize, me), device_id_type=MESH)

    dat[...] = jnp.zeros((16, LANES), F32)
    dat[:, 0:SURVEYS] = jnp.broadcast_to(datum[...], (16, SURVEYS))

    for n, copy in loads:
        if n < 3:
            copy.wait()

    def pack_strip(b, _):
        r = pl.ds(pl.multiple_of(b * 32, 32), 32)
        lane = lanes_of(32)
        first, last = 0, tiles - 1
        low = jnp.where(lane < 4, ids[first, r, :].astype(F32), pltpu.roll(cq[first, r, :], 4, 1))
        low = jnp.where(lane < 8, low, pltpu.roll(obs[first, r, :], 8, 1))
        high = jnp.where(lane >= 124, ids[last, r, :].astype(F32), pltpu.roll(cq[last, r, :], LANES - 4, 1))
        high = jnp.where(lane >= 120, high, pltpu.roll(obs[last, r, :], LANES - 8, 1))
        bes[0, r, :] = jnp.where(lane < 64, low, high)
        return 0

    lax.fori_loop(0, rows // 32, pack_strip, 0, unroll=4)
    span = min(rows, LANES)
    for b in range(rows // span):
        strip_send[b] = bes[0, b * span : (b + 1) * span, :].T

    pl.semaphore_wait(barrier, along + zsize - 2)

    def strip_copy(side):
        at = pl.ds(0, 16) if side == 0 else pl.ds(112, 16)
        return pltpu.make_async_remote_copy(
            strip_send.at[:, at, :],
            strip_recv.at[:, at, :],
            strip_ss.at[side],
            strip_rs.at[side],
            device_id=(zi, me - 1 if side == 0 else me + 1),
            device_id_type=MESH,
        )

    has = (me > 0, me < along - 1)
    for side in range(2):

        @pl.when(has[side])
        def _():
            strip_copy(side).start()

    def make_onehot(g, _):
        sub = lax.broadcasted_iota(I32, (8, LANES), 0)
        for t in range(tiles):
            block = ids[t, pl.ds(pl.multiple_of(g * 32, 32), 32), :] & 7
            for r in range(0, 32, 2):
                pair = [
                    jnp.where(jnp.broadcast_to(block[r + i : r + i + 1, :], (8, LANES)) == sub, 1.0, 0.0)
                    for i in range(2)
                ]
                onehot[g, r * 8 : r * 8 + 16, t * LANES : (t + 1) * LANES] = jnp.concatenate(pair, 0).astype(BF16)
        return 0

    lax.fori_loop(0, groups, make_onehot, 0, unroll=4)

    def profile(values, hid, g):
        high = values.astype(BF16)
        low = (values - high.astype(F32)).astype(BF16)
        zero = jnp.zeros_like(high)
        match = [hid == h for h in range(5)]
        left = jnp.concatenate([jnp.where(m, p, zero) for p in (high, low) for m in match], 0)
        full = lax.dot_general(left, onehot[g], (((1,), (1,)), ((), ())), preferred_element_type=F32)
        full = full[:160] + full[160:]
        own = lax.broadcasted_iota(I32, (32, 256), 0) == lax.broadcasted_iota(I32, (32, 256), 1) // 8
        sums = [jnp.sum(jnp.where(own, full[32 * h : 32 * h + 32], 0.0), axis=0, keepdims=True) for h in range(5)]
        return jnp.concatenate(sums + [jnp.zeros((3, 256), F32)], 0)

    def high_bits(r):
        return jnp.concatenate([(ids[t, r, :] >> 3) & 7 for t in range(tiles)], 1)

    def put_profile(n, g, sums):
        hist[n, 2 * g] = sums[:, :LANES]
        hist[n, 2 * g + 1] = sums[:, LANES:]

    def part_copy(n, step):
        to = partner(step)
        return pltpu.make_async_remote_copy(
            hist.at[n, to],
            parts.at[n, slot_of(step)],
            part_ss.at[n],
            part_rs.at[n],
            device_id=(zi, to),
            device_id_type=MESH,
        )

    def all_parts(n):
        return pltpu.make_async_remote_copy(
            hist.at[n, pl.ds(1, along - 1)],
            parts.at[n, pl.ds(1, along - 1)],
            part_ss.at[n],
            part_rs.at[n],
            device_id=(zi, me),
            device_id_type=MESH,
        )

    def z_copy(n, k):
        return pltpu.make_async_remote_copy(
            zsend.at[n],
            zrecv.at[n, zsize - k],
            z_ss.at[n],
            z_rs.at[n],
            device_id=((zi + k) % zsize, me),
            device_id_type=MESH,
        )

    def all_z(n):
        return pltpu.make_async_remote_copy(
            zrecv.at[n, pl.ds(1, zsize - 1)],
            zrecv.at[n, pl.ds(1, zsize - 1)],
            z_ss.at[n],
            z_rs.at[n],
            device_id=(zi, me),
            device_id_type=MESH,
        )

    def send_profile(n):
        total = jnp.sum(hist[n], axis=0)
        zsend[n] = total
        zrecv[n, 0] = total
        for k in sorted(range(1, zsize), key=lambda k: -torus_distance(k, zsize)):
            z_copy(n, k).start()
        for step in steps:
            part_copy(n, step).start()
        parts[n, 0] = hist[n, me]

    def summed_parts(n):
        all_parts(n).wait_recv()
        return jnp.sum(parts[n], axis=0)

    def summed_z(n):
        all_z(n).wait_recv()
        return jnp.broadcast_to(jnp.sum(jnp.sum(zrecv[n], axis=0), keepdims=True), (8, LANES))

    for n, copy in loads:
        if n == 3:
            copy.wait()

    def weights(g, _):
        r = pl.ds(pl.multiple_of(g * 32, 32), 32)
        values = []
        for t in range(tiles):
            value = mask[t, r, :].astype(F32) * cq[t, r, :]
            w[t, r, :] = value
            values.append(value)
        put_profile(SWEEPS, g, profile(jnp.concatenate(values, 1), high_bits(r), g))
        return 0

    lax.fori_loop(0, groups, weights, 0, unroll=8)
    send_profile(SWEEPS)

    for side in range(2):

        @pl.when(has[1 - side])
        def _():
            strip_copy(side).wait_recv()

    for b in range(rows // span):
        bes[0, b * span : (b + 1) * span, :] = strip_recv[b].T

    def prepare(b, _):
        r = pl.ds(pl.multiple_of(b * 16, 16), 16)
        lane = lanes_of(16)
        upper = jnp.where(lax.broadcasted_iota(I32, (16, LANES), 0) >= 8, 64, 0)
        got = bes[0, r, :]
        edge_low, edge_high = lane < DEPTH, lane >= LANES - DEPTH
        ids[tiles, r, :] = jnp.where(edge_low | edge_high, got, 0.0).astype(I32)
        cq[tiles, r, :] = jnp.where(
            edge_low, pltpu.roll(got, LANES - 4, 1), jnp.where(edge_high, pltpu.roll(got, 4, 1), 0.0)
        )
        obs[tiles, r, :] = jnp.where(
            edge_low, pltpu.roll(got, LANES - 8, 1), jnp.where(edge_high, pltpu.roll(got, 8, 1), 0.0)
        )
        for t in range(tiles + 1):
            survey = ids[t, r, :]
            weight = cq[t, r, :]
            seen = obs[t, r, :] + lane_take(dat[...], survey)
            inverse = 1.0 / (weight + 4.0 * smooth_weight)
            if t == tiles:
                inside = weight > 0.0
                seen = jnp.where(inside, seen, 0.0)
                inverse = jnp.where(inside, inverse, 0.0)
            share = weight * inverse
            ids[t, r, :] = survey + upper
            obs[t, r, :] = seen
            q[t, r, :] = inverse
            cq[t, r, :] = share
            pp[t, r, :] = share * seen
            mm[t, pl.ds(pl.multiple_of(b * 16 + 8, 8), 16), :] = seen
        return 0

    lax.fori_loop(0, rows // 16, prepare, 0, unroll=4)

    def row_copy(k, side):
        at, to = ((8, rows + 8), (rows + 7, 7))[side]
        return pltpu.make_async_remote_copy(
            mm.at[:, pl.ds(at, 1), :],
            mm.at[:, pl.ds(to, 1), :],
            row_ss.at[k, side],
            row_rs.at[k, side],
            device_id=(zi - 1 if side == 0 else zi + 1, me),
            device_id_type=MESH,
        )

    above = (zi > 0, zi < zsize - 1)

    def send_rows(k):
        for side in range(2):

            @pl.when(above[side])
            def _():
                row_copy(k, side).start()

    def wait_rows(k):
        for side in range(2):

            @pl.when(above[1 - side])
            def _():
                row_copy(k, side).wait_recv()

        for side in range(2):

            @pl.when(above[side])
            def _():
                row_copy(k, side).wait_send()

    send_rows(0)

    def stencil_group(k, g):
        first = g * 32
        r = pl.ds(pl.multiple_of(first, 32), 32)
        lane = lanes_of(32)
        now = [mm[t, pl.ds(pl.multiple_of(first + 8, 8), 32), :] for t in range(tiles + 1)]
        gaps = []
        for t in range(tiles + 1):
            before, after = now[(t - 1) % (tiles + 1)], now[(t + 1) % (tiles + 1)]
            value = mm[t, pl.ds(first + 7, 32), :] + mm[t, pl.ds(first + 9, 32), :]
            value += pltpu.roll(jnp.where(lane == LANES - 1, before, now[t]), 1, 1)
            value += pltpu.roll(jnp.where(lane == 0, after, now[t]), LANES - 1, 1)
            bes[t, r, :] = value
            if t < tiles:
                gaps.append(w[t, r, :] * (0.25 * value - obs[t, r, :]))
        put_profile(k, g, profile(jnp.concatenate(gaps, 1), high_bits(r), g))

    def local_update(k, alpha, beta):
        def block(b, _):
            r = pl.ds(pl.multiple_of(b * 32, 32), 32)
            for t in range(tiles + 1):
                now = mm[t, pl.ds(pl.multiple_of(b * 32 + 8, 8), 32), :]
                value = beta * (pp[t, r, :] + q[t, r, :] * bes[t, r, :] - now)
                if k > 0:
                    value += alpha * d[t, r, :]
                d[t, r, :] = value
            return 0

        lax.fori_loop(0, rows // 32, block, 0, unroll=4)

    def owner_tile(k):
        sums = summed_parts(k)
        if k == 0:
            floor[...] = jnp.maximum(summed_parts(SWEEPS), 1.0)
        share = sums / floor[...]
        lane = lanes_of(8)
        sub = lax.broadcasted_iota(I32, (8, LANES), 0)
        index = 8 * (sub + jnp.where(lane >= 64, 8, 0)) + (lane & 7)
        kind = (lane & 63) >> 3
        tile = jnp.zeros((8, LANES), F32)
        for h in range(5):
            tile = jnp.where(kind == h, lane_take(jnp.broadcast_to(share[h : h + 1], (8, LANES)), index), tile)
        tile = jnp.where(kind == 5, summed_z(k), tile)
        if k == 0:
            tile = jnp.where(kind > 5, summed_z(SWEEPS), tile)
        table[k, me] = tile

    def table_copy(k, step):
        return pltpu.make_async_remote_copy(
            table.at[k, me],
            table.at[k, me],
            table_ss.at[k],
            table_rs.at[k],
            device_id=(zi, partner(step)),
            device_id_type=MESH,
        )

    def all_table(k):
        return pltpu.make_async_remote_copy(
            table.at[k, pl.ds(0, along - 1)],
            table.at[k, pl.ds(0, along - 1)],
            table_ss.at[k],
            table_rs.at[k],
            device_id=(zi, me),
            device_id_type=MESH,
        )

    stores = []
    for k, (alpha, beta) in enumerate(coefficients()):
        last = k == SWEEPS - 1

        def inner(g, _, k=k):
            stencil_group(k, g)
            return 0

        lax.fori_loop(1, groups - 1, inner, 0, unroll=7)
        wait_rows(k)
        stencil_group(k, 0)
        stencil_group(k, groups - 1)
        send_profile(k)
        local_update(k, alpha, beta)

        owner_tile(k)
        for step in steps:
            table_copy(k, step).start()
        all_table(k).wait_recv()

        whole = jnp.sum(table[k], axis=0)
        if k == 0:
            wtotal[...] = lane_take(whole, jnp.full((8, LANES), 48, I32)) + 1.0
        level = lane_take(whole, jnp.full((8, LANES), 40, I32)) / wtotal[...]
        level = jnp.concatenate([level, level], 0)

        def update(b, _, k=k, last=last, beta=beta, level=level):
            r = pl.ds(pl.multiple_of(b * 16, 16), 16)
            at = pl.ds(pl.multiple_of(b * 16 + 8, 8), 16)
            row_table = table[k, b]
            row_table = jnp.concatenate([row_table, row_table], 0) - level
            for t in range(tiles if last else tiles + 1):
                step = d[t, r, :] + beta * cq[t, r, :] * lane_take(row_table, ids[t, r, :])
                if not last:
                    d[t, r, :] = step
                mm[t, at, :] = mm[t, at, :] + step
            return 0

        if not last:
            update(0, 0)
            update(rows // 16 - 1, 0)
            send_rows(k + 1)
            lax.fori_loop(1, rows // 16 - 1, update, 0, unroll=5)
        else:
            chunks = 4
            for c in range(chunks):
                size = rows // chunks
                lax.fori_loop(c * size // 16, (c + 1) * size // 16, update, 0, unroll=4)
                for t in range(tiles):
                    copy = pltpu.make_async_copy(
                        mm.at[t, pl.ds(8 + c * size, size), :],
                        merged_out.at[pl.ds(c * size, size), pl.ds(t * LANES, LANES)],
                        store_sem.at[c, t],
                    )
                    copy.start()
                    stores.append(copy)
            for b in range(rows // span):
                pieces = []
                for o in range(b * span // 16, (b + 1) * span // 16):
                    piece = table[k, o] - level[:8]
                    pieces += [piece, pltpu.roll(piece, 64, 1)]
                offs[:, b * span : (b + 1) * span] = jnp.concatenate(pieces, 0).T[:SURVEYS]
            copy = pltpu.make_async_copy(offs, offsets_out, store_sem.at[chunks, 0])
            copy.start()
            stores.append(copy)

    for side in range(2):

        @pl.when(has[side])
        def _():
            strip_copy(side).wait_send()

    for n in range(SWEEPS + 1):
        all_parts(n).wait_send()
        all_z(n).wait_send()
    for k in range(SWEEPS):
        all_table(k).wait_send()
    for copy in stores:
        copy.wait()


def solution(mesh):
    zsize, along = mesh.shape["strip"], mesh.shape["along"]
    dims = (4, 4, 2) if along == 32 else (1, along // 2, 2)

    def on_device(heights, confidence, survey_ids, seam_mask, datum):
        rows, cols = heights.shape
        assert rows == 16 * along and cols % 256 == 0
        tiles = cols // LANES
        wide = (tiles + 1, rows, LANES)
        narrow = (tiles, rows, LANES)
        span = min(rows, LANES)
        strip = (rows // span, LANES, span)
        dma = pltpu.SemaphoreType.DMA
        scratch = [
            pltpu.VMEM((tiles + 1, rows + 16, LANES), F32),
            pltpu.VMEM(wide, I32),
            pltpu.VMEM(wide, F32),
            pltpu.VMEM(wide, F32),
            pltpu.VMEM(wide, F32),
            pltpu.VMEM(wide, F32),
            pltpu.VMEM(narrow, F32),
            pltpu.VMEM(wide, F32),
            pltpu.VMEM(wide, F32),
            pltpu.VMEM(narrow, I32),
            pltpu.VMEM((rows // 32, 256, cols), BF16),
            pltpu.VMEM((16, LANES), F32),
            pltpu.VMEM(strip, F32),
            pltpu.VMEM(strip, F32),
            pltpu.VMEM((SWEEPS + 1, along, 8, LANES), F32),
            pltpu.VMEM((SWEEPS + 1, along, 8, LANES), F32),
            pltpu.VMEM((8, LANES), F32),
            pltpu.VMEM((SWEEPS + 1, 8, LANES), F32),
            pltpu.VMEM((SWEEPS + 1, zsize, 8, LANES), F32),
            pltpu.VMEM((SWEEPS, along, 8, LANES), F32),
            pltpu.VMEM((8, LANES), F32),
            pltpu.VMEM((SURVEYS, rows), F32),
            dma((4, tiles)),
            dma((5, tiles)),
            dma((2,)),
            dma((2,)),
            dma((SWEEPS, 2)),
            dma((SWEEPS, 2)),
            dma((SWEEPS + 1,)),
            dma((SWEEPS + 1,)),
            dma((SWEEPS + 1,)),
            dma((SWEEPS + 1,)),
            dma((SWEEPS,)),
            dma((SWEEPS,)),
        ]
        return pl.pallas_call(
            functools.partial(kernel, zsize, dims),
            out_shape=(
                jax.ShapeDtypeStruct((rows, cols), F32),
                jax.ShapeDtypeStruct((SURVEYS, rows), F32),
            ),
            in_specs=[pl.BlockSpec(memory_space=pl.ANY)] * 4 + [pl.BlockSpec(memory_space=pltpu.VMEM)],
            out_specs=(pl.BlockSpec(memory_space=pl.ANY), pl.BlockSpec(memory_space=pl.ANY)),
            scratch_shapes=scratch,
            compiler_params=pltpu.CompilerParams(
                collective_id=0, has_side_effects=True, vmem_limit_bytes=60 * 1024 * 1024
            ),
        )(heights, confidence, survey_ids, seam_mask, datum.reshape(1, SURVEYS))

    return jax.shard_map(
        on_device,
        mesh=mesh,
        in_specs=(P("strip", "along"),) * 4 + (P(),),
        out_specs=(P("strip", "along"), P(None, "strip")),
        check_vma=False,
    )
```

```python
import functools

import jax
import jax.numpy as jnp
from jax import lax
from jax.experimental import pallas as pl
from jax.experimental.pallas import tpu as pltpu
from jax.sharding import PartitionSpec as P

SURVEYS = 40
SWEEPS = 4

smooth_weight = 1.0
centre_value = 1.05
half_width = 0.95

LANES = 128
DEPTH = 4
MESH = pl.DeviceIdType.MESH
F32 = jnp.float32
BF16 = jnp.bfloat16
I32 = jnp.int32


def coefficients():
    sigma_value = centre_value / half_width
    ratio_now = 1.0 / sigma_value
    pairs = [(0.0, 1.0 / centre_value)]
    for _ in range(SWEEPS - 1):
        ratio_next = 1.0 / (2.0 * sigma_value - ratio_now)
        pairs.append((ratio_next * ratio_now, 2.0 * ratio_next / half_width))
        ratio_now = ratio_next
    return pairs


def torus_distance(step, size):
    return min(step % size, (-step) % size)


def lane_take(values, index):
    return jnp.take_along_axis(values, index, axis=1, mode="promise_in_bounds")


def lanes_of(rows):
    return lax.broadcasted_iota(I32, (rows, LANES), 1)


def kernel(
    zsize,
    dims,
    heights,
    confidence,
    survey_ids,
    seam_mask,
    datum,
    merged_out,
    offsets_out,
    mm,
    ids,
    obs,
    q,
    cq,
    pp,
    w,
    d,
    bes,
    mask,
    onehot,
    datum_row,
    dat,
    strip_send,
    strip_recv,
    hist,
    parts,
    floor,
    zsend,
    zrecv,
    table,
    wtotal,
    offs,
    load_sem,
    store_sem,
    strip_ss,
    strip_rs,
    row_ss,
    row_rs,
    part_ss,
    part_rs,
    z_ss,
    z_rs,
    table_ss,
    table_rs,
):
    ny, nx, nc = dims
    along = ny * nx * nc
    rows, cols = heights.shape
    tiles = cols // LANES
    groups = rows // 32
    zi = lax.axis_index("strip")
    me = lax.axis_index("along")
    my_y, my_x, my_c = me // (nx * nc), (me // nc) % nx, me % nc

    steps = [(a, b, c) for a in range(ny) for b in range(nx) for c in range(nc)]
    steps = sorted(steps[1:], key=lambda s: -(torus_distance(s[0], ny) + torus_distance(s[1], nx) + 0.3 * s[2]))

    def partner(step):
        a, b, c = step
        return (((my_y + a) % ny) * nx + (my_x + b) % nx) * nc + (my_c + c) % nc

    def slot_of(step):
        a, b, c = step
        return (((-a) % ny) * nx + (-b) % nx) * nc + (-c) % nc

    loads = []
    for t in range(tiles):
        for n, (src, dst) in enumerate(((survey_ids, ids), (confidence, cq), (heights, obs), (seam_mask, mask))):
            copy = pltpu.make_async_copy(src.at[:, pl.ds(t * LANES, LANES)], dst.at[t], load_sem.at[n, t])
            copy.start()
            loads.append((n, copy))

    datum_copy = pltpu.make_async_copy(datum, datum_row, load_sem.at[4, 0])
    datum_copy.start()

    mm[:, 0:8, :] = jnp.zeros((tiles + 1, 8, LANES), F32)
    mm[:, rows + 8 : rows + 16, :] = jnp.zeros((tiles + 1, 8, LANES), F32)
    strip_recv[...] = jnp.zeros(strip_recv.shape, F32)

    barrier = pltpu.get_barrier_semaphore()
    for step in steps:
        pl.semaphore_signal(barrier, inc=1, device_id=(zi, partner(step)), device_id_type=MESH)
    for k in range(1, zsize):
        pl.semaphore_signal(barrier, inc=1, device_id=((zi + k) % zsize, me), device_id_type=MESH)

    for n, copy in loads:
        if n < 3:
            copy.wait()
    datum_copy.wait()
    dat[...] = jnp.zeros((16, LANES), F32)
    dat[:, 0:SURVEYS] = jnp.broadcast_to(datum_row[...], (16, SURVEYS))

    def pack_strip(b, _):
        r = pl.ds(pl.multiple_of(b * 32, 32), 32)
        lane = lanes_of(32)
        first, last = 0, tiles - 1
        low = jnp.where(lane < 4, ids[first, r, :].astype(F32), pltpu.roll(cq[first, r, :], 4, 1))
        low = jnp.where(lane < 8, low, pltpu.roll(obs[first, r, :], 8, 1))
        high = jnp.where(lane >= 124, ids[last, r, :].astype(F32), pltpu.roll(cq[last, r, :], LANES - 4, 1))
        high = jnp.where(lane >= 120, high, pltpu.roll(obs[last, r, :], LANES - 8, 1))
        bes[0, r, :] = jnp.where(lane < 64, low, high)
        return 0

    lax.fori_loop(0, rows // 32, pack_strip, 0, unroll=4)
    span = min(rows, LANES)
    for b in range(rows // span):
        strip_send[b] = bes[0, b * span : (b + 1) * span, :].T

    pl.semaphore_wait(barrier, along + zsize - 2)

    def strip_copy(side):
        at = pl.ds(0, 16) if side == 0 else pl.ds(112, 16)
        return pltpu.make_async_remote_copy(
            strip_send.at[:, at, :],
            strip_recv.at[:, at, :],
            strip_ss.at[side],
            strip_rs.at[side],
            device_id=(zi, me - 1 if side == 0 else me + 1),
            device_id_type=MESH,
        )

    has = (me > 0, me < along - 1)
    for side in range(2):

        @pl.when(has[side])
        def _():
            strip_copy(side).start()

    def make_onehot(g):
        sub = lax.broadcasted_iota(I32, (8, LANES), 0)
        for t in range(tiles):
            block = ids[t, pl.ds(pl.multiple_of(g * 32, 32), 32), :] & 7
            for r in range(0, 32, 2):
                pair = [
                    jnp.where(jnp.broadcast_to(block[r + i : r + i + 1, :], (8, LANES)) == sub, 1.0, 0.0)
                    for i in range(2)
                ]
                onehot[g, r * 8 : r * 8 + 16, t * LANES : (t + 1) * LANES] = jnp.concatenate(pair, 0).astype(BF16)

    def profile(values, hid, g):
        high = values.astype(BF16)
        low = (values - high.astype(F32)).astype(BF16)
        zero = jnp.zeros_like(high)
        match = [hid == h for h in range(5)]
        left = jnp.concatenate([jnp.where(m, p, zero) for p in (high, low) for m in match], 0)
        full = lax.dot_general(left, onehot[g], (((1,), (1,)), ((), ())), preferred_element_type=F32)
        lane = lanes_of(8)
        sub = lax.broadcasted_iota(I32, (8, LANES), 0)
        own_row = (lane >> 3) & 7
        out = []
        for j in range(2):
            tile = jnp.zeros((8, LANES), F32)
            for h in range(5):
                value = 0.0
                for part in range(2):
                    at = (part * 5 + h) * 32 + 16 * j
                    pair = [full[at + 8 * i : at + 8 * i + 8, j * LANES : (j + 1) * LANES] for i in range(2)]
                    value += jnp.where(lane < 64, pair[0], pair[1])
                value = jnp.take_along_axis(value, own_row, axis=0, mode="promise_in_bounds")
                tile = jnp.where(sub == h, value, tile)
            out.append(tile)
        return out

    def high_bits(r):
        return jnp.concatenate([(ids[t, r, :] >> 3) & 7 for t in range(tiles)], 1)

    def put_profile(n, g, sums):
        hist[n, 2 * g] = sums[0]
        hist[n, 2 * g + 1] = sums[1]

    def part_copy(n, step):
        to = partner(step)
        return pltpu.make_async_remote_copy(
            hist.at[n, to],
            parts.at[n, slot_of(step)],
            part_ss.at[n],
            part_rs.at[n],
            device_id=(zi, to),
            device_id_type=MESH,
        )

    def all_parts(n):
        return pltpu.make_async_remote_copy(
            hist.at[n, pl.ds(1, along - 1)],
            parts.at[n, pl.ds(1, along - 1)],
            part_ss.at[n],
            part_rs.at[n],
            device_id=(zi, me),
            device_id_type=MESH,
        )

    def z_copy(n, k):
        return pltpu.make_async_remote_copy(
            zsend.at[n],
            zrecv.at[n, zsize - k],
            z_ss.at[n],
            z_rs.at[n],
            device_id=((zi + k) % zsize, me),
            device_id_type=MESH,
        )

    def all_z(n):
        return pltpu.make_async_remote_copy(
            zrecv.at[n, pl.ds(1, zsize - 1)],
            zrecv.at[n, pl.ds(1, zsize - 1)],
            z_ss.at[n],
            z_rs.at[n],
            device_id=(zi, me),
            device_id_type=MESH,
        )

    def send_profile(n):
        total = jnp.sum(hist[n], axis=0)
        zsend[n] = total
        zrecv[n, 0] = total
        for k in sorted(range(1, zsize), key=lambda k: -torus_distance(k, zsize)):
            z_copy(n, k).start()
        for step in steps:
            part_copy(n, step).start()
        parts[n, 0] = hist[n, me]

    def summed_parts(n):
        all_parts(n).wait_recv()
        return jnp.sum(parts[n], axis=0)

    def summed_z(n):
        all_z(n).wait_recv()
        return jnp.broadcast_to(jnp.sum(jnp.sum(zrecv[n], axis=0), keepdims=True), (8, LANES))

    for n, copy in loads:
        if n == 3:
            copy.wait()

    def row_copy(k, n, side):
        at, to = ((8, rows + 8), (rows + 7, 7))[side]
        which = pl.ds(0, tiles) if n == SWEEPS else pl.ds(tiles, 1) if k == 0 else pl.ds(0, tiles + 1)
        return pltpu.make_async_remote_copy(
            mm.at[which, pl.ds(at, 1), :],
            mm.at[which, pl.ds(to, 1), :],
            row_ss.at[n, side],
            row_rs.at[n, side],
            device_id=(zi - 1 if side == 0 else zi + 1, me),
            device_id_type=MESH,
        )

    above = (zi > 0, zi < zsize - 1)

    def send_rows(k, n):
        for side in range(2):

            @pl.when(above[side])
            def _():
                row_copy(k, n, side).start()

    def wait_rows(k, n):
        for side in range(2):

            @pl.when(above[1 - side])
            def _():
                row_copy(k, n, side).wait_recv()

        for side in range(2):

            @pl.when(above[side])
            def _():
                row_copy(k, n, side).wait_send()

    def prepare(g, t):
        r = pl.ds(pl.multiple_of(g * 32, 32), 32)
        upper = jnp.where(lax.broadcasted_iota(I32, (32, LANES), 0) & 8 > 0, 64, 0)
        survey = ids[t, r, :]
        weight = cq[t, r, :]
        seen = obs[t, r, :] + lane_take(jnp.concatenate([dat[...]] * 2, 0), survey)
        inverse = 1.0 / (weight + 4.0 * smooth_weight)
        if t == tiles:
            inside = weight > 0.0
            seen = jnp.where(inside, seen, 0.0)
            inverse = jnp.where(inside, inverse, 0.0)
        share = weight * inverse
        ids[t, r, :] = survey + upper
        obs[t, r, :] = seen
        q[t, r, :] = inverse
        cq[t, r, :] = share
        pp[t, r, :] = share * seen
        mm[t, pl.ds(pl.multiple_of(g * 32 + 8, 8), 32), :] = seen

    def start_group(g, _):
        r = pl.ds(pl.multiple_of(g * 32, 32), 32)
        make_onehot(g)
        values = []
        for t in range(tiles):
            value = mask[t, r, :].astype(F32) * cq[t, r, :]
            w[t, r, :] = value
            values.append(value)
        put_profile(SWEEPS, g, profile(jnp.concatenate(values, 1), high_bits(r), g))
        for t in range(tiles):
            prepare(g, t)
        return 0

    lax.fori_loop(0, groups, start_group, 0, unroll=4)
    send_rows(0, SWEEPS)
    send_profile(SWEEPS)

    for side in range(2):

        @pl.when(has[1 - side])
        def _():
            strip_copy(side).wait_recv()

    for b in range(rows // span):
        bes[0, b * span : (b + 1) * span, :] = strip_recv[b].T

    def unpack_strip(g, _):
        r = pl.ds(pl.multiple_of(g * 32, 32), 32)
        lane = lanes_of(32)
        got = bes[0, r, :]
        edge_low, edge_high = lane < DEPTH, lane >= LANES - DEPTH
        ids[tiles, r, :] = jnp.where(edge_low | edge_high, got, 0.0).astype(I32)
        cq[tiles, r, :] = jnp.where(
            edge_low, pltpu.roll(got, LANES - 4, 1), jnp.where(edge_high, pltpu.roll(got, 4, 1), 0.0)
        )
        obs[tiles, r, :] = jnp.where(
            edge_low, pltpu.roll(got, LANES - 8, 1), jnp.where(edge_high, pltpu.roll(got, 8, 1), 0.0)
        )
        prepare(g, tiles)
        return 0

    lax.fori_loop(0, groups, unpack_strip, 0, unroll=4)
    send_rows(0, 0)

    def stencil_group(k, g):
        first = g * 32
        r = pl.ds(pl.multiple_of(first, 32), 32)
        lane = lanes_of(32)
        now = [mm[t, pl.ds(pl.multiple_of(first + 8, 8), 32), :] for t in range(tiles + 1)]
        gaps = []
        for t in range(tiles + 1):
            before, after = now[(t - 1) % (tiles + 1)], now[(t + 1) % (tiles + 1)]
            value = mm[t, pl.ds(first + 7, 32), :] + mm[t, pl.ds(first + 9, 32), :]
            value += pltpu.roll(jnp.where(lane == LANES - 1, before, now[t]), 1, 1)
            value += pltpu.roll(jnp.where(lane == 0, after, now[t]), LANES - 1, 1)
            bes[t, r, :] = value
            if t < tiles:
                gaps.append(w[t, r, :] * (0.25 * value - obs[t, r, :]))
        put_profile(k, g, profile(jnp.concatenate(gaps, 1), high_bits(r), g))

    def local_update(k, alpha, beta):
        def block(b, _):
            r = pl.ds(pl.multiple_of(b * 32, 32), 32)
            for t in range(tiles + 1):
                now = mm[t, pl.ds(pl.multiple_of(b * 32 + 8, 8), 32), :]
                value = beta * (pp[t, r, :] + q[t, r, :] * bes[t, r, :] - now)
                if k > 0:
                    value += alpha * d[t, r, :]
                d[t, r, :] = value
            return 0

        lax.fori_loop(0, rows // 32, block, 0, unroll=4)

    def owner_tile(k):
        gap_total = summed_z(k)
        if k == 0:
            weight_total = summed_z(SWEEPS)
            floor[...] = 1.0 / jnp.maximum(summed_parts(SWEEPS), 1.0)
        share = summed_parts(k) * floor[...]
        lane = lanes_of(8)
        sub = lax.broadcasted_iota(I32, (8, LANES), 0)
        index = 8 * (sub + jnp.where(lane >= 64, 8, 0)) + (lane & 7)
        kind = (lane & 63) >> 3
        tile = jnp.zeros((8, LANES), F32)
        for h in range(5):
            tile = jnp.where(kind == h, lane_take(jnp.broadcast_to(share[h : h + 1], (8, LANES)), index), tile)
        tile = jnp.where(kind == 5, gap_total, tile)
        if k == 0:
            tile = jnp.where(kind > 5, weight_total, tile)
        table[k, me] = tile

    def table_copy(k, step):
        return pltpu.make_async_remote_copy(
            table.at[k, me],
            table.at[k, me],
            table_ss.at[k],
            table_rs.at[k],
            device_id=(zi, partner(step)),
            device_id_type=MESH,
        )

    def all_table(k):
        return pltpu.make_async_remote_copy(
            table.at[k, pl.ds(0, along - 1)],
            table.at[k, pl.ds(0, along - 1)],
            table_ss.at[k],
            table_rs.at[k],
            device_id=(zi, me),
            device_id_type=MESH,
        )

    def update_group(g, beta, level, last):
        r = pl.ds(pl.multiple_of(g * 32, 32), 32)
        at = pl.ds(pl.multiple_of(g * 32 + 8, 8), 32)
        row_table = [table[last, 2 * g + i] for i in (0, 0, 1, 1)]
        row_table = jnp.concatenate(row_table, 0) - level
        for t in range(tiles if last == SWEEPS - 1 else tiles + 1):
            step = d[t, r, :] + beta * cq[t, r, :] * lane_take(row_table, ids[t, r, :])
            if last < SWEEPS - 1:
                d[t, r, :] = step
            mm[t, at, :] = mm[t, at, :] + step

    stores = []
    level, before = None, None
    for k, (alpha, beta) in enumerate(coefficients()):
        if k == 0:

            def first(g, _):
                stencil_group(0, g)
                return 0

            lax.fori_loop(1, groups - 1, first, 0, unroll=14)
            wait_rows(0, SWEEPS)
            wait_rows(0, 0)
        else:
            update_group(0, before, level, k - 1)
            update_group(groups - 1, before, level, k - 1)
            send_rows(k, k)
            update_group(1, before, level, k - 1)

            def both(g, _, k=k, before=before, level=level):
                update_group(g + 1, before, level, k - 1)
                stencil_group(k, g)
                return 0

            lax.fori_loop(1, groups - 2, both, 0, unroll=13)
            stencil_group(k, groups - 2)
            wait_rows(k, k)
        stencil_group(k, 0)
        stencil_group(k, groups - 1)
        send_profile(k)
        local_update(k, alpha, beta)

        owner_tile(k)
        for step in steps:
            table_copy(k, step).start()
        all_table(k).wait_recv()

        whole = jnp.sum(table[k], axis=0)
        if k == 0:
            wtotal[...] = lane_take(whole, jnp.full((8, LANES), 48, I32)) + 1.0
        level = lane_take(whole, jnp.full((8, LANES), 40, I32)) / wtotal[...]
        level = jnp.concatenate([level] * 4, 0)
        before = beta

    chunks = 4
    for c in range(chunks):
        size = rows // chunks

        def final(g, _, level=level):
            update_group(g, before, level, SWEEPS - 1)
            return 0

        lax.fori_loop(c * size // 32, (c + 1) * size // 32, final, 0, unroll=4)
        for t in range(tiles):
            copy = pltpu.make_async_copy(
                mm.at[t, pl.ds(8 + c * size, size), :],
                merged_out.at[pl.ds(c * size, size), pl.ds(t * LANES, LANES)],
                store_sem.at[c, t],
            )
            copy.start()
            stores.append(copy)
    for b in range(rows // span):
        pieces = []
        for o in range(b * span // 16, (b + 1) * span // 16):
            piece = table[SWEEPS - 1, o] - level[:8]
            pieces += [piece, pltpu.roll(piece, 64, 1)]
        offs[:, b * span : (b + 1) * span] = jnp.concatenate(pieces, 0).T[:SURVEYS]
    copy = pltpu.make_async_copy(offs, offsets_out, store_sem.at[chunks, 0])
    copy.start()
    stores.append(copy)

    for side in range(2):

        @pl.when(has[side])
        def _():
            strip_copy(side).wait_send()

    for n in range(SWEEPS + 1):
        all_parts(n).wait_send()
        all_z(n).wait_send()
    for k in range(SWEEPS):
        all_table(k).wait_send()
    for copy in stores:
        copy.wait()


def solution(mesh):
    zsize, along = mesh.shape["strip"], mesh.shape["along"]
    dims = (4, 4, 2) if along == 32 else (1, along // 2, 2)

    def on_device(heights, confidence, survey_ids, seam_mask, datum):
        rows, cols = heights.shape
        assert rows == 16 * along and cols % 256 == 0
        tiles = cols // LANES
        wide = (tiles + 1, rows, LANES)
        narrow = (tiles, rows, LANES)
        span = min(rows, LANES)
        strip = (rows // span, LANES, span)
        dma = pltpu.SemaphoreType.DMA
        scratch = [
            pltpu.VMEM((tiles + 1, rows + 16, LANES), F32),
            pltpu.VMEM(wide, I32),
            pltpu.VMEM(wide, F32),
            pltpu.VMEM(wide, F32),
            pltpu.VMEM(wide, F32),
            pltpu.VMEM(wide, F32),
            pltpu.VMEM(narrow, F32),
            pltpu.VMEM(wide, F32),
            pltpu.VMEM(wide, F32),
            pltpu.VMEM(narrow, I32),
            pltpu.VMEM((rows // 32, 256, cols), BF16),
            pltpu.VMEM((1, SURVEYS), F32),
            pltpu.VMEM((16, LANES), F32),
            pltpu.VMEM(strip, F32),
            pltpu.VMEM(strip, F32),
            pltpu.VMEM((SWEEPS + 1, along, 8, LANES), F32),
            pltpu.VMEM((SWEEPS + 1, along, 8, LANES), F32),
            pltpu.VMEM((8, LANES), F32),
            pltpu.VMEM((SWEEPS + 1, 8, LANES), F32),
            pltpu.VMEM((SWEEPS + 1, zsize, 8, LANES), F32),
            pltpu.VMEM((SWEEPS, along, 8, LANES), F32),
            pltpu.VMEM((8, LANES), F32),
            pltpu.VMEM((SURVEYS, rows), F32),
            dma((5, tiles)),
            dma((5, tiles)),
            dma((2,)),
            dma((2,)),
            dma((SWEEPS + 1, 2)),
            dma((SWEEPS + 1, 2)),
            dma((SWEEPS + 1,)),
            dma((SWEEPS + 1,)),
            dma((SWEEPS + 1,)),
            dma((SWEEPS + 1,)),
            dma((SWEEPS,)),
            dma((SWEEPS,)),
        ]
        return pl.pallas_call(
            functools.partial(kernel, zsize, dims),
            out_shape=(
                jax.ShapeDtypeStruct((rows, cols), F32),
                jax.ShapeDtypeStruct((SURVEYS, rows), F32),
            ),
            in_specs=[pl.BlockSpec(memory_space=pl.ANY)] * 5,
            out_specs=(pl.BlockSpec(memory_space=pl.ANY), pl.BlockSpec(memory_space=pl.ANY)),
            scratch_shapes=scratch,
            compiler_params=pltpu.CompilerParams(
                collective_id=0, has_side_effects=True, vmem_limit_bytes=52 * 1024 * 1024
            ),
        )(heights, confidence, survey_ids, seam_mask, datum.reshape(1, SURVEYS))

    return jax.shard_map(
        on_device,
        mesh=mesh,
        in_specs=(P("strip", "along"),) * 4 + (P(),),
        out_specs=(P("strip", "along"), P(None, "strip")),
        check_vma=False,
    )
```

```python
import functools

import jax
import jax.numpy as jnp
from jax import lax
from jax.experimental import pallas as pl
from jax.experimental.pallas import tpu as pltpu
from jax.sharding import PartitionSpec as P

SURVEYS = 40
SWEEPS = 4

smooth_weight = 1.0
centre_value = 1.05
half_width = 0.95

LANES = 128
HIGH = 5
DEPTH = 4
MESH = pl.DeviceIdType.MESH
F32 = jnp.float32
BF16 = jnp.bfloat16
I32 = jnp.int32


def coefficients():
    sigma_value = centre_value / half_width
    ratio_now = 1.0 / sigma_value
    pairs = [(0.0, 1.0 / centre_value)]
    for _ in range(SWEEPS - 1):
        ratio_next = 1.0 / (2.0 * sigma_value - ratio_now)
        pairs.append((ratio_next * ratio_now, 2.0 * ratio_next / half_width))
        ratio_now = ratio_next
    return pairs


def torus_distance(step, size):
    return min(step % size, (-step) % size)


def lane_take(values, index):
    return jnp.take_along_axis(values, index, axis=1, mode="promise_in_bounds")


def lanes_of(rows):
    return lax.broadcasted_iota(I32, (rows, LANES), 1)


def kernel(
    zsize,
    dims,
    heights,
    confidence,
    survey_ids,
    seam_mask,
    datum,
    merged_out,
    offsets_out,
    mm,
    ids,
    obs,
    q,
    cq,
    pp,
    w,
    d,
    bes,
    mask,
    onehot,
    datum_row,
    dat,
    strip_send,
    strip_recv,
    hist,
    hist_first,
    parts,
    parts_first,
    floor,
    zsend,
    zrecv,
    table,
    wtotal,
    offs,
    row_cq,
    row_ids,
    base_send,
    base_recv,
    halo_table,
    load_sem,
    store_sem,
    strip_ss,
    strip_rs,
    row_ss,
    row_rs,
    part_ss,
    part_rs,
    z_ss,
    z_rs,
    table_ss,
    table_rs,
    halo_ss,
    halo_rs,
):
    ny, nx, nc = dims
    along = ny * nx * nc
    rows, cols = heights.shape
    tiles = cols // LANES
    groups = rows // 32
    zi = lax.axis_index("strip")
    me = lax.axis_index("along")
    my_y, my_x, my_c = me // (nx * nc), (me // nc) % nx, me % nc

    steps = [(a, b, c) for a in range(ny) for b in range(nx) for c in range(nc)]
    steps = sorted(steps[1:], key=lambda s: -(torus_distance(s[0], ny) + torus_distance(s[1], nx) + 0.3 * s[2]))

    def partner(step):
        a, b, c = step
        return (((my_y + a) % ny) * nx + (my_x + b) % nx) * nc + (my_c + c) % nc

    def slot_of(step):
        a, b, c = step
        return (((-a) % ny) * nx + (-b) % nx) * nc + (-c) % nc

    loads = {}
    load_order = [0, tiles - 1] + list(range(1, tiles - 1))
    for t in load_order:
        for n, (src, dst) in enumerate(((survey_ids, ids), (confidence, cq), (heights, obs), (seam_mask, mask))):
            copy = pltpu.make_async_copy(src.at[:, pl.ds(t * LANES, LANES)], dst.at[t], load_sem.at[n, t])
            copy.start()
            loads[n, t] = copy

    datum_copy = pltpu.make_async_copy(datum, datum_row, load_sem.at[4, 0])
    datum_copy.start()

    mm[:, 0:8, :] = jnp.zeros((tiles + 1, 8, LANES), F32)
    mm[:, rows + 8 : rows + 16, :] = jnp.zeros((tiles + 1, 8, LANES), F32)
    strip_recv[...] = jnp.zeros(strip_recv.shape, F32)
    row_cq[...] = jnp.zeros(row_cq.shape, F32)
    row_ids[...] = jnp.zeros(row_ids.shape, I32)
    base_recv[...] = jnp.zeros(base_recv.shape, F32)
    halo_table[...] = jnp.zeros(halo_table.shape, F32)

    barrier = pltpu.get_barrier_semaphore()
    for step in steps:
        pl.semaphore_signal(barrier, inc=1, device_id=(zi, partner(step)), device_id_type=MESH)
    for k in range(1, zsize):
        pl.semaphore_signal(barrier, inc=1, device_id=((zi + k) % zsize, me), device_id_type=MESH)

    for t in (0, tiles - 1):
        for n in range(3):
            loads[n, t].wait()
    datum_copy.wait()
    dat[...] = jnp.zeros((16, LANES), F32)
    dat[:, 0:SURVEYS] = jnp.broadcast_to(datum_row[...], (16, SURVEYS))

    def pack_strip(b, _):
        r = pl.ds(pl.multiple_of(b * 32, 32), 32)
        lane = lanes_of(32)
        first, last = 0, tiles - 1
        low = jnp.where(lane < 4, ids[first, r, :].astype(F32), pltpu.roll(cq[first, r, :], 4, 1))
        low = jnp.where(lane < 8, low, pltpu.roll(obs[first, r, :], 8, 1))
        high = jnp.where(lane >= 124, ids[last, r, :].astype(F32), pltpu.roll(cq[last, r, :], LANES - 4, 1))
        high = jnp.where(lane >= 120, high, pltpu.roll(obs[last, r, :], LANES - 8, 1))
        bes[0, r, :] = jnp.where(lane < 64, low, high)
        return 0

    lax.fori_loop(0, rows // 32, pack_strip, 0, unroll=4)
    span = min(rows, LANES)
    for b in range(rows // span):
        strip_send[b] = bes[0, b * span : (b + 1) * span, :].T

    pl.semaphore_wait(barrier, along + zsize - 2)

    def strip_copy(side):
        at = pl.ds(0, 16) if side == 0 else pl.ds(112, 16)
        return pltpu.make_async_remote_copy(
            strip_send.at[:, at, :],
            strip_recv.at[:, at, :],
            strip_ss.at[side],
            strip_rs.at[side],
            device_id=(zi, me - 1 if side == 0 else me + 1),
            device_id_type=MESH,
        )

    has = (me > 0, me < along - 1)
    for side in range(2):

        @pl.when(has[side])
        def _():
            strip_copy(side).start()

    def make_onehot(g):
        sub = lax.broadcasted_iota(I32, (8, LANES), 0)
        for t in range(tiles):
            block = ids[t, pl.ds(pl.multiple_of(g * 32, 32), 32), :] & 7
            for r in range(0, 32, 2):
                pair = [
                    jnp.where(jnp.broadcast_to(block[r + i : r + i + 1, :], (8, LANES)) == sub, 1.0, 0.0)
                    for i in range(2)
                ]
                onehot[g, r * 8 : r * 8 + 16, t * LANES : (t + 1) * LANES] = jnp.concatenate(pair, 0).astype(BF16)

    def profile(arrays, hid, g):
        pieces = []
        for values in arrays:
            high = values.astype(BF16)
            pieces += [high, (values - high.astype(F32)).astype(BF16)]
        zero = jnp.zeros_like(pieces[0])
        match = [hid == h for h in range(HIGH)]
        left = jnp.concatenate([jnp.where(m, p, zero) for p in pieces for m in match], 0)
        full = lax.dot_general(left, onehot[g], (((1,), (1,)), ((), ())), preferred_element_type=F32)
        lane = lanes_of(8)
        sub = lax.broadcasted_iota(I32, (8, LANES), 0)
        own_row = (lane >> 3) & 7
        out = []
        for n in range(len(arrays)):
            for j in range(2):
                tile = jnp.zeros((8, LANES), F32)
                for h in range(HIGH):
                    value = 0.0
                    for part in range(2):
                        at = ((2 * n + part) * HIGH + h) * 32 + 16 * j
                        pair = [full[at + 8 * i : at + 8 * i + 8, j * LANES : (j + 1) * LANES] for i in range(2)]
                        value += jnp.where(lane < 64, pair[0], pair[1])
                    value = jnp.take_along_axis(value, own_row, axis=0, mode="promise_in_bounds")
                    tile = jnp.where(sub == h, value, tile)
                out.append(tile)
        return out

    def high_bits(r):
        return jnp.concatenate([(ids[t, r, :] >> 3) & 7 for t in range(tiles)], 1)

    used = pl.ds(0, HIGH)

    def put_profile(k, g, sums):
        for j in range(2):
            if k == 0:
                hist_first[2 * g + j, 0] = sums[j]
                hist_first[2 * g + j, 1] = sums[2 + j]
            else:
                hist[k, 2 * g + j] = sums[j]

    def part_copy(k, to, slot):
        return pltpu.make_async_remote_copy(
            hist_first.at[to, :, used] if k == 0 else hist.at[k, to, used],
            parts_first.at[slot, :, used] if k == 0 else parts.at[k, slot, used],
            part_ss.at[k],
            part_rs.at[k],
            device_id=(zi, to),
            device_id_type=MESH,
        )

    def all_parts(k):
        many = pl.ds(1, along - 1)
        return pltpu.make_async_remote_copy(
            hist_first.at[many, :, used] if k == 0 else hist.at[k, many, used],
            parts_first.at[many, :, used] if k == 0 else parts.at[k, many, used],
            part_ss.at[k],
            part_rs.at[k],
            device_id=(zi, me),
            device_id_type=MESH,
        )

    def z_copy(n, k):
        return pltpu.make_async_remote_copy(
            zsend.at[n],
            zrecv.at[n, zsize - k],
            z_ss.at[n],
            z_rs.at[n],
            device_id=((zi + k) % zsize, me),
            device_id_type=MESH,
        )

    def all_z(n):
        return pltpu.make_async_remote_copy(
            zrecv.at[n, pl.ds(1, zsize - 1)],
            zrecv.at[n, pl.ds(1, zsize - 1)],
            z_ss.at[n],
            z_rs.at[n],
            device_id=(zi, me),
            device_id_type=MESH,
        )

    def send_total(n, total):
        zsend[n] = total
        zrecv[n, 0] = total
        for k in sorted(range(1, zsize), key=lambda k: -torus_distance(k, zsize)):
            z_copy(n, k).start()

    def send_inner(k):
        for step in steps:
            to = partner(step)

            @pl.when((to >= 2) & (to < along - 2))
            def _():
                part_copy(k, to, slot_of(step)).start()

    def send_outer(k):
        for to in (0, 1, along - 2, along - 1):
            y, x, c = to // (nx * nc), (to // nc) % nx, to % nc
            slot = (((my_y + ny - y) % ny) * nx + (my_x + nx - x) % nx) * nc + (my_c + nc - c) % nc

            @pl.when(me != to)
            def _():
                part_copy(k, to, slot).start()

        if k == 0:
            parts_first[0, :, 0:HIGH, :] = hist_first[me, :, 0:HIGH, :]
            send_total(0, jnp.sum(hist_first[:, 0], axis=0))
            send_total(SWEEPS, jnp.sum(hist_first[:, 1], axis=0))
        else:
            parts[k, 0, 0:HIGH, :] = hist[k, me, 0:HIGH, :]
            send_total(k, jnp.sum(hist[k], axis=0))

    def summed_z(n):
        all_z(n).wait_recv()
        return jnp.broadcast_to(jnp.sum(jnp.sum(zrecv[n], axis=0), keepdims=True), (8, LANES))

    above = (zi > 0, zi < zsize - 1)

    def row_copies(n, side):
        own, far = ((0, rows + 8), (rows - 8, 0))[side]
        own, far, shifted = pl.ds(own, 8), pl.ds(far, 8), pl.ds(own + 8, 8)
        every = pl.ds(0, tiles + 1)
        if n == 0:
            pairs = [(mm.at[pl.ds(0, tiles), shifted, :], mm.at[pl.ds(0, tiles), far, :])]
        elif n == 1:
            pairs = [
                (mm.at[pl.ds(tiles, 1), shifted, :], mm.at[pl.ds(tiles, 1), far, :]),
                (cq.at[every, own, :], row_cq.at[1 - side]),
                (ids.at[every, own, :], row_ids.at[1 - side]),
            ]
        else:
            pairs = [(base_send.at[n - 2, side], base_recv.at[n - 2, 1 - side])]
        return [
            pltpu.make_async_remote_copy(
                src,
                dst,
                row_ss.at[n, side, i],
                row_rs.at[n, side, i],
                device_id=(zi - 1 if side == 0 else zi + 1, me),
                device_id_type=MESH,
            )
            for i, (src, dst) in enumerate(pairs)
        ]

    def send_rows(n):
        for side in range(2):

            @pl.when(above[side])
            def _():
                for copy in row_copies(n, side):
                    copy.start()

    def wait_rows(n):
        for side in range(2):

            @pl.when(above[1 - side])
            def _():
                for copy in row_copies(n, side):
                    copy.wait_recv()

    def rows_sent(n):
        for side in range(2):

            @pl.when(above[side])
            def _():
                for copy in row_copies(n, side):
                    copy.wait_send()

    def prepare(g, t):
        r = pl.ds(pl.multiple_of(g * 32, 32), 32)
        upper = jnp.where(lax.broadcasted_iota(I32, (32, LANES), 0) & 8 > 0, 64, 0)
        survey = ids[t, r, :]
        weight = cq[t, r, :]
        seen = obs[t, r, :] + lane_take(jnp.concatenate([dat[...]] * 2, 0), survey)
        inverse = 1.0 / (weight + 4.0 * smooth_weight)
        if t == tiles:
            inside = weight > 0.0
            seen = jnp.where(inside, seen, 0.0)
            inverse = jnp.where(inside, inverse, 0.0)
        share = weight * inverse
        if t < tiles:
            w[t, r, :] = weight
        ids[t, r, :] = survey + upper
        obs[t, r, :] = seen
        q[t, r, :] = inverse
        cq[t, r, :] = share
        pp[t, r, :] = share * seen
        mm[t, pl.ds(pl.multiple_of(g * 32 + 8, 8), 32), :] = seen

    for t in load_order:

        def start_group(g, _, t=t):
            prepare(g, t)
            return 0

        for n in range(3):
            if t not in (0, tiles - 1):
                loads[n, t].wait()
        lax.fori_loop(0, groups, start_group, 0, unroll=8)
    send_rows(0)
    for t in range(tiles):
        loads[3, t].wait()

    for side in range(2):

        @pl.when(has[1 - side])
        def _():
            strip_copy(side).wait_recv()

    for b in range(rows // span):
        bes[0, b * span : (b + 1) * span, :] = strip_recv[b].T

    def unpack_strip(g, _):
        r = pl.ds(pl.multiple_of(g * 32, 32), 32)
        lane = lanes_of(32)
        got = bes[0, r, :]
        edge_low, edge_high = lane < DEPTH, lane >= LANES - DEPTH
        ids[tiles, r, :] = jnp.where(edge_low | edge_high, got, 0.0).astype(I32)
        cq[tiles, r, :] = jnp.where(
            edge_low, pltpu.roll(got, LANES - 4, 1), jnp.where(edge_high, pltpu.roll(got, 4, 1), 0.0)
        )
        obs[tiles, r, :] = jnp.where(
            edge_low, pltpu.roll(got, LANES - 8, 1), jnp.where(edge_high, pltpu.roll(got, 8, 1), 0.0)
        )
        prepare(g, tiles)
        return 0

    lax.fori_loop(0, groups, unpack_strip, 0, unroll=8)
    send_rows(1)

    def stencil_group(k, g):
        first = g * 32
        r = pl.ds(pl.multiple_of(first, 32), 32)
        lane = lanes_of(32)
        now = [mm[t, pl.ds(pl.multiple_of(first + 8, 8), 32), :] for t in range(tiles + 1)]
        gaps, weights = [], []
        for t in range(tiles + 1):
            before, after = now[(t - 1) % (tiles + 1)], now[(t + 1) % (tiles + 1)]
            value = mm[t, pl.ds(first + 7, 32), :] + mm[t, pl.ds(first + 9, 32), :]
            value += pltpu.roll(jnp.where(lane == LANES - 1, before, now[t]), 1, 1)
            value += pltpu.roll(jnp.where(lane == 0, after, now[t]), LANES - 1, 1)
            bes[t, r, :] = value
            if t < tiles:
                if k == 0:
                    weight = mask[t, r, :].astype(F32) * w[t, r, :]
                    w[t, r, :] = weight
                    weights.append(weight)
                gaps.append(w[t, r, :] * (0.25 * value - obs[t, r, :]))
        arrays = [jnp.concatenate(gaps, 1)]
        if k == 0:
            make_onehot(g)
            arrays.append(jnp.concatenate(weights, 1))
        put_profile(k, g, profile(arrays, high_bits(r), g))

    def local_update(k, alpha, beta):
        def block(b, _):
            r = pl.ds(pl.multiple_of(b * 32, 32), 32)
            for t in range(tiles + 1):
                now = mm[t, pl.ds(pl.multiple_of(b * 32 + 8, 8), 32), :]
                value = beta * (pp[t, r, :] + q[t, r, :] * bes[t, r, :] - now)
                if k > 0:
                    value += alpha * d[t, r, :]
                d[t, r, :] = value
            return 0

        lax.fori_loop(0, rows // 32, block, 0, unroll=4)

    def owner_tile(k):
        gap_total = summed_z(k)
        if k == 0:
            weight_total = summed_z(SWEEPS)
            all_parts(0).wait_recv()
            floor[...] = 1.0 / jnp.maximum(jnp.sum(parts_first[:, 1, 0:HIGH, :], axis=0), 1.0)
            share = jnp.sum(parts_first[:, 0, 0:HIGH, :], axis=0) * floor[...]
        else:
            all_parts(k).wait_recv()
            share = jnp.sum(parts[k, :, 0:HIGH, :], axis=0) * floor[...]
        lane = lanes_of(8)
        sub = lax.broadcasted_iota(I32, (8, LANES), 0)
        index = 8 * (sub + jnp.where(lane >= 64, 8, 0)) + (lane & 7)
        kind = (lane & 63) >> 3
        tile = jnp.zeros((8, LANES), F32)
        for h in range(HIGH):
            tile = jnp.where(kind == h, lane_take(jnp.broadcast_to(share[h : h + 1], (8, LANES)), index), tile)
        tile = jnp.where(kind == 5, gap_total, tile)
        if k == 0:
            tile = jnp.where(kind > 5, weight_total, tile)
        table[k, me] = tile

    kind = jnp.where(me == 0, 1, jnp.where(me == along - 1, 2, 0))
    enders = (me == 0, me == along - 1)

    def table_copy(k, step):
        return pltpu.make_async_remote_copy(
            table.at[k, me],
            table.at[k, me],
            table_ss.at[k],
            table_rs.at[k, kind],
            device_id=(zi, partner(step)),
            device_id_type=MESH,
        )

    def some_table(k, count, which):
        return pltpu.make_async_remote_copy(
            table.at[k, pl.ds(0, count)],
            table.at[k, pl.ds(0, count)],
            table_ss.at[k],
            table_rs.at[k, which],
            device_id=(zi, me),
            device_id_type=MESH,
        )

    def hand_on(k, side):
        return pltpu.make_async_remote_copy(
            table.at[k, 0 if side == 0 else along - 1],
            halo_table.at[k, 1 - side],
            halo_ss.at[k, side],
            halo_rs.at[k, 1 - side],
            device_id=(zi - 1 if side == 0 else zi + 1, me),
            device_id_type=MESH,
        )

    def receive_tables(k, last):
        for side in range(2):

            @pl.when(jnp.logical_not(enders[side]))
            def _():
                some_table(k, 1, 1 + side).wait_recv()

            if not last:

                @pl.when(above[side])
                def _():
                    hand_on(k, side).start()

        ender = enders[0] | enders[1]

        @pl.when(ender)
        def _():
            some_table(k, along - 2, 0).wait_recv()

        @pl.when(jnp.logical_not(ender))
        def _():
            some_table(k, along - 2 - 1, 0).wait_recv()

    def update_halo(k, beta, level):
        wait_rows(k + 2)
        for side in range(2):

            @pl.when(above[side])
            def _():
                hand_on(k, 1 - side).wait_recv()

            row_table = halo_table[k, side]
            at = (0, rows + 8)[side]
            for t in range(tiles + 1):
                step = beta * row_cq[side, t] * (lane_take(row_table, row_ids[side, t]) - level[:8])
                mm[t, at : at + 8, :] = base_recv[k, side, t] + step

    def update_group(g, beta, level, last):
        r = pl.ds(pl.multiple_of(g * 32, 32), 32)
        at = pl.ds(pl.multiple_of(g * 32 + 8, 8), 32)
        row_table = [table[last, 2 * g + i] for i in (0, 0, 1, 1)]
        row_table = jnp.concatenate(row_table, 0)
        for t in range(tiles if last == SWEEPS - 1 else tiles + 1):
            spread = lane_take(row_table, ids[t, r, :]) - level
            step = d[t, r, :] + beta * cq[t, r, :] * spread
            if last < SWEEPS - 1:
                d[t, r, :] = step
            mm[t, at, :] = mm[t, at, :] + step

    stores = []
    level, before = None, None
    for k, (alpha, beta) in enumerate(coefficients()):
        last = k == SWEEPS - 1
        if k == 0:

            def first(g, _):
                stencil_group(0, g)
                return 0

            lax.fori_loop(1, groups - 1, first, 0, unroll=14)
            send_inner(0)
            for n in range(2):
                wait_rows(n)
            for n in range(2):
                rows_sent(n)
        else:
            update_group(0, before, level, k - 1)
            update_group(1, before, level, k - 1)

            def both(g, _, k=k, before=before, level=level):
                update_group(g + 1, before, level, k - 1)
                stencil_group(k, g)
                return 0

            lax.fori_loop(1, groups - 1, both, 0, unroll=14)
            send_inner(k)
            update_halo(k - 1, before, level)
        stencil_group(k, 0)
        stencil_group(k, groups - 1)
        send_outer(k)
        local_update(k, alpha, beta)
        if not last:
            for side, at in enumerate((0, rows - 8)):
                for t in range(tiles + 1):
                    base_send[k, side, t] = mm[t, at + 8 : at + 16, :] + d[t, at : at + 8, :]
            send_rows(k + 2)

        owner_tile(k)
        for step in steps:
            table_copy(k, step).start()
        receive_tables(k, last)

        whole = jnp.sum(table[k], axis=0)
        if k == 0:
            wtotal[...] = lane_take(whole, jnp.full((8, LANES), 48, I32)) + 1.0
        level = lane_take(whole, jnp.full((8, LANES), 40, I32)) / wtotal[...]
        level = jnp.concatenate([level] * 4, 0)
        before = beta

    chunks = 4
    for c in range(chunks):
        size = rows // chunks

        def final(g, _, level=level):
            update_group(g, before, level, SWEEPS - 1)
            return 0

        lax.fori_loop(c * size // 32, (c + 1) * size // 32, final, 0, unroll=4)
        for t in range(tiles):
            copy = pltpu.make_async_copy(
                mm.at[t, pl.ds(8 + c * size, size), :],
                merged_out.at[pl.ds(c * size, size), pl.ds(t * LANES, LANES)],
                store_sem.at[c, t],
            )
            copy.start()
            stores.append(copy)
    for b in range(rows // span):
        pieces = []
        for o in range(b * span // 16, (b + 1) * span // 16):
            piece = table[SWEEPS - 1, o] - level[:8]
            pieces += [piece, pltpu.roll(piece, 64, 1)]
        offs[:, b * span : (b + 1) * span] = jnp.concatenate(pieces, 0).T[:SURVEYS]
    copy = pltpu.make_async_copy(offs, offsets_out, store_sem.at[chunks, 0])
    copy.start()
    stores.append(copy)

    for side in range(2):

        @pl.when(has[side])
        def _():
            strip_copy(side).wait_send()

    for n in range(SWEEPS + 1):
        all_z(n).wait_send()
    for k in range(SWEEPS):
        all_parts(k).wait_send()
        some_table(k, along - 1, 0).wait_send()
    for k in range(SWEEPS - 1):
        rows_sent(k + 2)
        for side in range(2):

            @pl.when(above[side])
            def _():
                hand_on(k, side).wait_send()

    for copy in stores:
        copy.wait()


def solution(mesh):
    zsize, along = mesh.shape["strip"], mesh.shape["along"]
    dims = (4, 4, 2) if along == 32 else (1, along // 2, 2)

    def on_device(heights, confidence, survey_ids, seam_mask, datum):
        rows, cols = heights.shape
        assert rows == 16 * along and cols % 256 == 0
        tiles = cols // LANES
        wide = (tiles + 1, rows, LANES)
        narrow = (tiles, rows, LANES)
        span = min(rows, LANES)
        strip = (rows // span, LANES, span)
        dma = pltpu.SemaphoreType.DMA
        scratch = [
            pltpu.VMEM((tiles + 1, rows + 16, LANES), F32),
            pltpu.VMEM(wide, I32),
            pltpu.VMEM(wide, F32),
            pltpu.VMEM(wide, F32),
            pltpu.VMEM(wide, F32),
            pltpu.VMEM(wide, F32),
            pltpu.VMEM(narrow, F32),
            pltpu.VMEM(wide, F32),
            pltpu.VMEM(wide, F32),
            pltpu.VMEM(narrow, I32),
            pltpu.VMEM((rows // 32, 256, cols), BF16),
            pltpu.VMEM((1, SURVEYS), F32),
            pltpu.VMEM((16, LANES), F32),
            pltpu.VMEM(strip, F32),
            pltpu.VMEM(strip, F32),
            pltpu.VMEM((SWEEPS, along, 8, LANES), F32),
            pltpu.VMEM((along, 2, 8, LANES), F32),
            pltpu.VMEM((SWEEPS, along, 8, LANES), F32),
            pltpu.VMEM((along, 2, 8, LANES), F32),
            pltpu.VMEM((HIGH, LANES), F32),
            pltpu.VMEM((SWEEPS + 1, 8, LANES), F32),
            pltpu.VMEM((SWEEPS + 1, zsize, 8, LANES), F32),
            pltpu.VMEM((SWEEPS, along, 8, LANES), F32),
            pltpu.VMEM((8, LANES), F32),
            pltpu.VMEM((SURVEYS, rows), F32),
            pltpu.VMEM((2, tiles + 1, 8, LANES), F32),
            pltpu.VMEM((2, tiles + 1, 8, LANES), I32),
            pltpu.VMEM((SWEEPS - 1, 2, tiles + 1, 8, LANES), F32),
            pltpu.VMEM((SWEEPS - 1, 2, tiles + 1, 8, LANES), F32),
            pltpu.VMEM((SWEEPS - 1, 2, 8, LANES), F32),
            dma((5, tiles)),
            dma((5, tiles)),
            dma((2,)),
            dma((2,)),
            dma((SWEEPS + 1, 2, 3)),
            dma((SWEEPS + 1, 2, 3)),
            dma((SWEEPS,)),
            dma((SWEEPS,)),
            dma((SWEEPS + 1,)),
            dma((SWEEPS + 1,)),
            dma((SWEEPS,)),
            dma((SWEEPS, 3)),
            dma((SWEEPS - 1, 2)),
            dma((SWEEPS - 1, 2)),
        ]
        return pl.pallas_call(
            functools.partial(kernel, zsize, dims),
            out_shape=(
                jax.ShapeDtypeStruct((rows, cols), F32),
                jax.ShapeDtypeStruct((SURVEYS, rows), F32),
            ),
            in_specs=[pl.BlockSpec(memory_space=pl.ANY)] * 5,
            out_specs=(pl.BlockSpec(memory_space=pl.ANY), pl.BlockSpec(memory_space=pl.ANY)),
            scratch_shapes=scratch,
            compiler_params=pltpu.CompilerParams(
                collective_id=0, has_side_effects=True, vmem_limit_bytes=52 * 1024 * 1024
            ),
        )(heights, confidence, survey_ids, seam_mask, datum.reshape(1, SURVEYS))

    return jax.shard_map(
        on_device,
        mesh=mesh,
        in_specs=(P("strip", "along"),) * 4 + (P(),),
        out_specs=(P("strip", "along"), P(None, "strip")),
        check_vma=False,
    )
```

```python
import functools

import jax
import jax.numpy as jnp
from jax import lax
from jax.experimental import pallas as pl
from jax.experimental.pallas import tpu as pltpu
from jax.sharding import PartitionSpec as P

SURVEYS = 40
SWEEPS = 4

smooth_weight = 1.0
centre_value = 1.05
half_width = 0.95

LANES = 128
HIGH = 5
DEPTH = 4
MESH = pl.DeviceIdType.MESH
F32 = jnp.float32
BF16 = jnp.bfloat16
I32 = jnp.int32


def coefficients():
    sigma_value = centre_value / half_width
    ratio_now = 1.0 / sigma_value
    pairs = [(0.0, 1.0 / centre_value)]
    for _ in range(SWEEPS - 1):
        ratio_next = 1.0 / (2.0 * sigma_value - ratio_now)
        pairs.append((ratio_next * ratio_now, 2.0 * ratio_next / half_width))
        ratio_now = ratio_next
    return pairs


def torus_distance(step, size):
    return min(step % size, (-step) % size)


def lane_take(values, index):
    return jnp.take_along_axis(values, index, axis=1, mode="promise_in_bounds")


def lanes_of(rows):
    return lax.broadcasted_iota(I32, (rows, LANES), 1)


def kernel(
    zsize,
    dims,
    heights,
    confidence,
    survey_ids,
    seam_mask,
    datum,
    merged_out,
    offsets_out,
    mm,
    ids,
    obs,
    q,
    cq,
    pp,
    w,
    d,
    bes,
    mask,
    onehot,
    datum_row,
    dat,
    strip_send,
    strip_recv,
    hist,
    hist_first,
    parts,
    parts_first,
    floor,
    zsend,
    zrecv,
    table,
    wtotal,
    offs,
    row_cq,
    row_ids,
    base_send,
    base_recv,
    halo_table,
    extra,
    extra_first,
    extra_floor,
    load_sem,
    store_sem,
    strip_ss,
    strip_rs,
    row_ss,
    row_rs,
    part_ss,
    part_rs,
    z_ss,
    z_rs,
    table_ss,
    table_rs,
    halo_ss,
    halo_rs,
    extra_ss,
    extra_rs,
):
    ny, nx, nc = dims
    along = ny * nx * nc
    rows, cols = heights.shape
    tiles = cols // LANES
    groups = rows // 32
    zi = lax.axis_index("strip")
    me = lax.axis_index("along")
    my_y, my_x, my_c = me // (nx * nc), (me // nc) % nx, me % nc

    steps = [(a, b, c) for a in range(ny) for b in range(nx) for c in range(nc)]
    steps = sorted(steps[1:], key=lambda s: -(torus_distance(s[0], ny) + torus_distance(s[1], nx) + 0.3 * s[2]))

    def turned(value, size):
        return [jnp.where(value + a >= size, value + a - size, value + a) for a in range(size)]

    ys, xs, cs = turned(my_y, ny), turned(my_x, nx), turned(my_c, nc)
    partners = {(a, b, c): (ys[a] * nx + xs[b]) * nc + cs[c] for a, b, c in [(0, 0, 0)] + steps}

    def partner(step):
        return partners[step]

    def slot_of(step):
        a, b, c = step
        return (((-a) % ny) * nx + (-b) % nx) * nc + (-c) % nc

    loads = {}
    load_order = [0, tiles - 1] + list(range(1, tiles - 1))
    for t in load_order:
        for n, (src, dst) in enumerate(((survey_ids, ids), (confidence, cq), (heights, obs), (seam_mask, mask))):
            copy = pltpu.make_async_copy(src.at[:, pl.ds(t * LANES, LANES)], dst.at[t], load_sem.at[n, t])
            copy.start()
            loads[n, t] = copy

    datum_copy = pltpu.make_async_copy(datum, datum_row, load_sem.at[4, 0])
    datum_copy.start()

    mm[:, 0:8, :] = jnp.zeros((tiles + 1, 8, LANES), F32)
    mm[:, rows + 8 : rows + 16, :] = jnp.zeros((tiles + 1, 8, LANES), F32)
    strip_recv[...] = jnp.zeros(strip_recv.shape, F32)
    row_cq[...] = jnp.zeros(row_cq.shape, F32)
    row_ids[...] = jnp.zeros(row_ids.shape, I32)
    base_recv[...] = jnp.zeros(base_recv.shape, F32)
    halo_table[...] = jnp.zeros(halo_table.shape, F32)

    barrier = pltpu.get_barrier_semaphore()
    for step in steps:
        pl.semaphore_signal(barrier, inc=1, device_id=(zi, partner(step)), device_id_type=MESH)
    for k in range(1, zsize):
        pl.semaphore_signal(barrier, inc=1, device_id=((zi + k) % zsize, me), device_id_type=MESH)

    for side in range(2):
        inside = zi > 0 if side == 0 else zi < zsize - 1

        @pl.when(inside & (me == (0 if side == 0 else along - 1)))
        def _():
            for step in steps:
                to = (zi - 1 if side == 0 else zi + 1, partner(step))
                pl.semaphore_signal(barrier, inc=1, device_id=to, device_id_type=MESH)


    for t in (0, tiles - 1):
        for n in range(3):
            loads[n, t].wait()
    datum_copy.wait()
    dat[...] = jnp.zeros((16, LANES), F32)
    dat[:, 0:SURVEYS] = jnp.broadcast_to(datum_row[...], (16, SURVEYS))

    def pack_strip(b, _):
        r = pl.ds(pl.multiple_of(b * 32, 32), 32)
        lane = lanes_of(32)
        first, last = 0, tiles - 1
        low = jnp.where(lane < 4, ids[first, r, :].astype(F32), pltpu.roll(cq[first, r, :], 4, 1))
        low = jnp.where(lane < 8, low, pltpu.roll(obs[first, r, :], 8, 1))
        high = jnp.where(lane >= 124, ids[last, r, :].astype(F32), pltpu.roll(cq[last, r, :], LANES - 4, 1))
        high = jnp.where(lane >= 120, high, pltpu.roll(obs[last, r, :], LANES - 8, 1))
        bes[0, r, :] = jnp.where(lane < 64, low, high)
        return 0

    lax.fori_loop(0, rows // 32, pack_strip, 0, unroll=4)
    span = min(rows, LANES)
    for b in range(rows // span):
        strip_send[b] = bes[0, b * span : (b + 1) * span, :].T

    greeted = jnp.where((zi > 0) & (me != along - 1), 1, 0) + jnp.where((zi < zsize - 1) & (me != 0), 1, 0)
    pl.semaphore_wait(barrier, along + zsize - 2 + greeted)


    def strip_copy(side):
        at = pl.ds(0, 16) if side == 0 else pl.ds(112, 16)
        return pltpu.make_async_remote_copy(
            strip_send.at[:, at, :],
            strip_recv.at[:, at, :],
            strip_ss.at[side],
            strip_rs.at[side],
            device_id=(zi, me - 1 if side == 0 else me + 1),
            device_id_type=MESH,
        )

    has = (me > 0, me < along - 1)
    for side in range(2):

        @pl.when(has[side])
        def _():
            strip_copy(side).start()

    def make_onehot(g):
        sub = lax.broadcasted_iota(I32, (8, LANES), 0)
        for t in range(tiles):
            block = ids[t, pl.ds(pl.multiple_of(g * 32, 32), 32), :] & 7
            for r in range(0, 32, 2):
                pair = [
                    jnp.where(jnp.broadcast_to(block[r + i : r + i + 1, :], (8, LANES)) == sub, 1.0, 0.0)
                    for i in range(2)
                ]
                onehot[g, r * 8 : r * 8 + 16, t * LANES : (t + 1) * LANES] = jnp.concatenate(pair, 0).astype(BF16)

    def profile(arrays, hid, g):
        pieces = []
        for values in arrays:
            high = values.astype(BF16)
            pieces += [high, (values - high.astype(F32)).astype(BF16)]
        zero = jnp.zeros_like(pieces[0])
        match = [hid == h for h in range(HIGH)]
        left = jnp.concatenate([jnp.where(m, p, zero) for p in pieces for m in match], 0)
        full = lax.dot_general(left, onehot[g], (((1,), (1,)), ((), ())), preferred_element_type=F32)
        lane = lanes_of(8)
        sub = lax.broadcasted_iota(I32, (8, LANES), 0)
        own_row = (lane >> 3) & 7
        out = []
        for n in range(len(arrays)):
            for j in range(2):
                tile = jnp.zeros((8, LANES), F32)
                for h in range(HIGH):
                    value = 0.0
                    for part in range(2):
                        at = ((2 * n + part) * HIGH + h) * 32 + 16 * j
                        pair = [full[at + 8 * i : at + 8 * i + 8, j * LANES : (j + 1) * LANES] for i in range(2)]
                        value += jnp.where(lane < 64, pair[0], pair[1])
                    value = jnp.take_along_axis(value, own_row, axis=0, mode="promise_in_bounds")
                    tile = jnp.where(sub == h, value, tile)
                out.append(tile)
        return out

    def high_bits(r):
        return jnp.concatenate([(ids[t, r, :] >> 3) & 7 for t in range(tiles)], 1)

    used = pl.ds(0, HIGH)

    def put_profile(k, g, sums):
        for j in range(2):
            if k == 0:
                hist_first[2 * g + j, 0] = sums[j]
                hist_first[2 * g + j, 1] = sums[2 + j]
            else:
                hist[k, 2 * g + j] = sums[j]

    def part_copy(k, to, slot):
        return pltpu.make_async_remote_copy(
            hist_first.at[to, :, used] if k == 0 else hist.at[k, to, used],
            parts_first.at[slot, :, used] if k == 0 else parts.at[k, slot, used],
            part_ss.at[k],
            part_rs.at[k],
            device_id=(zi, to),
            device_id_type=MESH,
        )

    def all_parts(k):
        many = pl.ds(1, along - 1)
        return pltpu.make_async_remote_copy(
            hist_first.at[many, :, used] if k == 0 else hist.at[k, many, used],
            parts_first.at[many, :, used] if k == 0 else parts.at[k, many, used],
            part_ss.at[k],
            part_rs.at[k],
            device_id=(zi, me),
            device_id_type=MESH,
        )

    def z_copy(n, k):
        return pltpu.make_async_remote_copy(
            zsend.at[n],
            zrecv.at[n, zsize - k],
            z_ss.at[n],
            z_rs.at[n],
            device_id=((zi + k) % zsize, me),
            device_id_type=MESH,
        )

    def all_z(n):
        return pltpu.make_async_remote_copy(
            zrecv.at[n, pl.ds(1, zsize - 1)],
            zrecv.at[n, pl.ds(1, zsize - 1)],
            z_ss.at[n],
            z_rs.at[n],
            device_id=(zi, me),
            device_id_type=MESH,
        )

    def send_total(n, total):
        zsend[n] = total
        zrecv[n, 0] = total
        for k in sorted(range(1, zsize), key=lambda k: -torus_distance(k, zsize)):
            z_copy(n, k).start()

    def send_inner(k):
        for step in steps:
            to = partner(step)

            @pl.when((to >= 2) & (to < along - 2))
            def _():
                part_copy(k, to, slot_of(step)).start()

    def send_outer(k):
        for to in (0, 1, along - 2, along - 1):
            y, x, c = to // (nx * nc), (to // nc) % nx, to % nc
            slot = (((my_y + ny - y) % ny) * nx + (my_x + nx - x) % nx) * nc + (my_c + nc - c) % nc

            @pl.when(me != to)
            def _():
                part_copy(k, to, slot).start()

        if k == 0:
            parts_first[0, :, 0:HIGH, :] = hist_first[me, :, 0:HIGH, :]
            send_total(0, jnp.sum(hist_first[:, 0], axis=0))
            send_total(SWEEPS, jnp.sum(hist_first[:, 1], axis=0))
        else:
            parts[k, 0, 0:HIGH, :] = hist[k, me, 0:HIGH, :]
            send_total(k, jnp.sum(hist[k], axis=0))

    def summed_z(n):
        all_z(n).wait_recv()
        return jnp.broadcast_to(jnp.sum(jnp.sum(zrecv[n], axis=0), keepdims=True), (8, LANES))

    above = (zi > 0, zi < zsize - 1)

    def row_copies(n, side):
        own, far = ((0, rows + 8), (rows - 8, 0))[side]
        own, far, shifted = pl.ds(own, 8), pl.ds(far, 8), pl.ds(own + 8, 8)
        every = pl.ds(0, tiles + 1)
        if n == 0:
            pairs = [(mm.at[pl.ds(0, tiles), shifted, :], mm.at[pl.ds(0, tiles), far, :])]
        elif n == 1:
            pairs = [
                (mm.at[pl.ds(tiles, 1), shifted, :], mm.at[pl.ds(tiles, 1), far, :]),
                (cq.at[every, own, :], row_cq.at[1 - side]),
                (ids.at[every, own, :], row_ids.at[1 - side]),
            ]
        else:
            pairs = [(base_send.at[n - 2, side], base_recv.at[n - 2, 1 - side])]
        return [
            pltpu.make_async_remote_copy(
                src,
                dst,
                row_ss.at[n, side, i],
                row_rs.at[n, side, i],
                device_id=(zi - 1 if side == 0 else zi + 1, me),
                device_id_type=MESH,
            )
            for i, (src, dst) in enumerate(pairs)
        ]

    def send_rows(n):
        for side in range(2):

            @pl.when(above[side])
            def _():
                for copy in row_copies(n, side):
                    copy.start()

    def wait_rows(n):
        for side in range(2):

            @pl.when(above[1 - side])
            def _():
                for copy in row_copies(n, side):
                    copy.wait_recv()

    def rows_sent(n):
        for side in range(2):

            @pl.when(above[side])
            def _():
                for copy in row_copies(n, side):
                    copy.wait_send()

    def prepare(g, t):
        r = pl.ds(pl.multiple_of(g * 32, 32), 32)
        upper = jnp.where(lax.broadcasted_iota(I32, (32, LANES), 0) & 8 > 0, 64, 0)
        survey = ids[t, r, :]
        weight = cq[t, r, :]
        seen = obs[t, r, :] + lane_take(jnp.concatenate([dat[...]] * 2, 0), survey)
        inverse = 1.0 / (weight + 4.0 * smooth_weight)
        if t == tiles:
            inside = weight > 0.0
            seen = jnp.where(inside, seen, 0.0)
            inverse = jnp.where(inside, inverse, 0.0)
        share = weight * inverse
        if t < tiles:
            w[t, r, :] = weight
        ids[t, r, :] = survey + upper
        obs[t, r, :] = seen
        q[t, r, :] = inverse
        cq[t, r, :] = share
        pp[t, r, :] = share * seen
        mm[t, pl.ds(pl.multiple_of(g * 32 + 8, 8), 32), :] = seen

    for t in load_order:

        def start_group(g, _, t=t):
            prepare(g, t)
            return 0

        for n in range(3):
            if t not in (0, tiles - 1):
                loads[n, t].wait()
        lax.fori_loop(0, groups, start_group, 0, unroll=8)
    send_rows(0)
    def own_onehot(g, _):
        make_onehot(g)
        return 0

    lax.fori_loop(0, groups, own_onehot, 0, unroll=8)
    for t in range(tiles):
        loads[3, t].wait()

    for side in range(2):

        @pl.when(has[1 - side])
        def _():
            strip_copy(side).wait_recv()

    def unpack_strip(g, _):
        r = pl.ds(pl.multiple_of(g * 32, 32), 32)
        lane = lanes_of(32)
        got = bes[0, r, :]
        edge_low, edge_high = lane < DEPTH, lane >= LANES - DEPTH
        ids[tiles, r, :] = jnp.where(edge_low | edge_high, got, 0.0).astype(I32)
        cq[tiles, r, :] = jnp.where(
            edge_low, pltpu.roll(got, LANES - 4, 1), jnp.where(edge_high, pltpu.roll(got, 4, 1), 0.0)
        )
        obs[tiles, r, :] = jnp.where(
            edge_low, pltpu.roll(got, LANES - 8, 1), jnp.where(edge_high, pltpu.roll(got, 8, 1), 0.0)
        )
        prepare(g, tiles)
        return 0

    blocks = rows // span
    order = [0, blocks - 1] + list(range(1, blocks - 1)) if blocks > 1 else [0]
    for i, b in enumerate(order):
        bes[0, b * span : (b + 1) * span, :] = strip_recv[b].T
        if i == min(1, blocks - 1):
            unpack_strip(0, 0)
            unpack_strip(groups - 1, 0)
            send_rows(1)
    lax.fori_loop(1, groups - 1, unpack_strip, 0, unroll=7)

    def stencil_group(k, g):
        first = g * 32
        r = pl.ds(pl.multiple_of(first, 32), 32)
        lane = lanes_of(32)
        now = [mm[t, pl.ds(pl.multiple_of(first + 8, 8), 32), :] for t in range(tiles + 1)]
        gaps, weights = [], []
        for t in range(tiles + 1):
            before, after = now[(t - 1) % (tiles + 1)], now[(t + 1) % (tiles + 1)]
            value = mm[t, pl.ds(first + 7, 32), :] + mm[t, pl.ds(first + 9, 32), :]
            value += pltpu.roll(jnp.where(lane == LANES - 1, before, now[t]), 1, 1)
            value += pltpu.roll(jnp.where(lane == 0, after, now[t]), LANES - 1, 1)
            bes[t, r, :] = value
            if t < tiles:
                if k == 0:
                    weight = mask[t, r, :].astype(F32) * w[t, r, :]
                    w[t, r, :] = weight
                    weights.append(weight)
                gaps.append(w[t, r, :] * (0.25 * value - obs[t, r, :]))
        arrays = [jnp.concatenate(gaps, 1)]
        if k == 0:
            arrays.append(jnp.concatenate(weights, 1))
        put_profile(k, g, profile(arrays, high_bits(r), g))

    def local_update(k, alpha, beta):
        def block(b, _):
            r = pl.ds(pl.multiple_of(b * 32, 32), 32)
            for t in range(tiles + 1):
                now = mm[t, pl.ds(pl.multiple_of(b * 32 + 8, 8), 32), :]
                value = beta * (pp[t, r, :] + q[t, r, :] * bes[t, r, :] - now)
                if k > 0:
                    value += alpha * d[t, r, :]
                d[t, r, :] = value
            return 0

        lax.fori_loop(0, rows // 32, block, 0, unroll=4)

    def row_tile(share):
        lane = lanes_of(8)
        sub = lax.broadcasted_iota(I32, (8, LANES), 0)
        index = 8 * (sub + jnp.where(lane >= 64, 8, 0)) + (lane & 7)
        kind = (lane & 63) >> 3
        tile = jnp.zeros((8, LANES), F32)
        for h in range(HIGH):
            tile = jnp.where(kind == h, lane_take(jnp.broadcast_to(share[h : h + 1], (8, LANES)), index), tile)
        return tile

    def owner_tile(k):
        gap_total = summed_z(k)
        if k == 0:
            weight_total = summed_z(SWEEPS)
            all_parts(0).wait_recv()
            floor[...] = 1.0 / jnp.maximum(jnp.sum(parts_first[:, 1, 0:HIGH, :], axis=0), 1.0)
            share = jnp.sum(parts_first[:, 0, 0:HIGH, :], axis=0) * floor[...]
        else:
            all_parts(k).wait_recv()
            share = jnp.sum(parts[k, :, 0:HIGH, :], axis=0) * floor[...]
        kind = (lanes_of(8) & 63) >> 3
        tile = row_tile(share)
        tile = jnp.where(kind == 5, gap_total, tile)
        if k == 0:
            tile = jnp.where(kind > 5, weight_total, tile)
        table[k, me] = tile

    def table_copy(k, step):
        return pltpu.make_async_remote_copy(
            table.at[k, me],
            table.at[k, me],
            table_ss.at[k],
            table_rs.at[k],
            device_id=(zi, partner(step)),
            device_id_type=MESH,
        )

    def all_table(k):
        return pltpu.make_async_remote_copy(
            table.at[k, pl.ds(0, along - 1)],
            table.at[k, pl.ds(0, along - 1)],
            table_ss.at[k],
            table_rs.at[k],
            device_id=(zi, me),
            device_id_type=MESH,
        )

    enders = (me == 0, me == along - 1)

    def extra_copy(k, side):
        tile = 0 if side == 0 else along - 1
        return pltpu.make_async_remote_copy(
            hist_first.at[tile, :, used] if k == 0 else hist.at[k, tile, used],
            extra_first.at[1 - side, me, :, used] if k == 0 else extra.at[k, 1 - side, me, used],
            extra_ss.at[k, side],
            extra_rs.at[k, 1 - side],
            device_id=(zi - 1 if side == 0 else zi + 1, along - 1 if side == 0 else 0),
            device_id_type=MESH,
        )

    def send_extra(k):
        for side in range(2):

            @pl.when(above[side])
            def _():
                extra_copy(k, side).start()

    def all_extra(k, side):
        return pltpu.make_async_remote_copy(
            hist_first.at[:, :, used] if k == 0 else hist.at[k, :, used],
            extra_first.at[side, :, :, used] if k == 0 else extra.at[k, side, :, used],
            extra_ss.at[k, side],
            extra_rs.at[k, side],
            device_id=(zi, me),
            device_id_type=MESH,
        )

    def halo_table_copy(k, side, step):
        return pltpu.make_async_remote_copy(
            halo_table.at[k, side],
            halo_table.at[k, side],
            halo_ss.at[k, side],
            halo_rs.at[k, side],
            device_id=(zi, partner(step)),
            device_id_type=MESH,
        )

    def all_halo_table(k, side):
        return pltpu.make_async_remote_copy(
            table.at[k, pl.ds(0, along - 1)],
            table.at[k, pl.ds(0, along - 1)],
            halo_ss.at[k, side],
            halo_rs.at[k, side],
            device_id=(zi, me),
            device_id_type=MESH,
        )

    def extra_tiles(k):
        for side in range(2):

            @pl.when(above[side] & enders[side])
            def _():
                all_extra(k, side).wait_recv()
                if k == 0:
                    total = jnp.sum(extra_first[side, :, 1, 0:HIGH, :], axis=0)
                    extra_floor[...] = 1.0 / jnp.maximum(total, 1.0)
                    share = jnp.sum(extra_first[side, :, 0, 0:HIGH, :], axis=0)
                else:
                    share = jnp.sum(extra[k, side, :, 0:HIGH, :], axis=0)
                halo_table[k, side] = row_tile(share * extra_floor[...])
                for step in steps:
                    halo_table_copy(k, side, step).start()

    def update_halo(k, beta, level):
        wait_rows(k + 2)
        for side in range(2):

            @pl.when(above[side])
            def _():
                @pl.when(jnp.logical_not(enders[side]))
                def _():
                    halo_table_copy(k, side, (0, 0, 0)).wait_recv()


            row_table = halo_table[k, side]
            at = (0, rows + 8)[side]
            for t in range(tiles + 1):
                step = beta * row_cq[side, t] * (lane_take(row_table, row_ids[side, t]) - level[:8])
                mm[t, at : at + 8, :] = base_recv[k, side, t] + step

    def update_group(g, beta, level, last):
        r = pl.ds(pl.multiple_of(g * 32, 32), 32)
        at = pl.ds(pl.multiple_of(g * 32 + 8, 8), 32)
        row_table = [table[last, 2 * g + i] for i in (0, 0, 1, 1)]
        row_table = jnp.concatenate(row_table, 0)
        for t in range(tiles if last == SWEEPS - 1 else tiles + 1):
            spread = lane_take(row_table, ids[t, r, :]) - level
            step = d[t, r, :] + beta * cq[t, r, :] * spread
            if last < SWEEPS - 1:
                d[t, r, :] = step
            mm[t, at, :] = mm[t, at, :] + step

    stores = []
    level, before = None, None
    for k, (alpha, beta) in enumerate(coefficients()):
        last = k == SWEEPS - 1
        if k == 0:

            def first(g, _):
                stencil_group(0, g)
                return 0

            lax.fori_loop(1, groups - 1, first, 0, unroll=14)
            send_inner(0)
            for n in range(2):
                wait_rows(n)
            for n in range(2):
                rows_sent(n)
        else:
            update_group(0, before, level, k - 1)
            update_group(1, before, level, k - 1)

            def both(g, _, k=k, before=before, level=level):
                update_group(g + 1, before, level, k - 1)
                stencil_group(k, g)
                return 0

            lax.fori_loop(1, groups - 1, both, 0, unroll=14)
            send_inner(k)
            update_halo(k - 1, before, level)
        stencil_group(k, 0)
        stencil_group(k, groups - 1)
        if not last:
            send_extra(k)
        send_outer(k)
        local_update(k, alpha, beta)
        if not last:
            for side, at in enumerate((0, rows - 8)):
                for t in range(tiles + 1):
                    base_send[k, side, t] = mm[t, at + 8 : at + 16, :] + d[t, at : at + 8, :]
            send_rows(k + 2)

        owner_tile(k)
        for step in steps:
            table_copy(k, step).start()
        if not last:
            extra_tiles(k)
        all_table(k).wait_recv()

        whole = jnp.sum(table[k], axis=0)
        if k == 0:
            wtotal[...] = lane_take(whole, jnp.full((8, LANES), 48, I32)) + 1.0
        level = lane_take(whole, jnp.full((8, LANES), 40, I32)) / wtotal[...]
        level = jnp.concatenate([level] * 4, 0)
        before = beta

    chunks = 4
    for b in range(rows // span):
        pieces = []
        for o in range(b * span // 16, (b + 1) * span // 16):
            piece = table[SWEEPS - 1, o] - level[:8]
            pieces += [piece, pltpu.roll(piece, 64, 1)]
        offs[:, b * span : (b + 1) * span] = jnp.concatenate(pieces, 0).T[:SURVEYS]
    copy = pltpu.make_async_copy(offs, offsets_out, store_sem.at[chunks, 0])
    copy.start()
    stores.append(copy)

    for c in range(chunks):
        size = rows // chunks

        def final(g, _, level=level):
            update_group(g, before, level, SWEEPS - 1)
            return 0

        lax.fori_loop(c * size // 32, (c + 1) * size // 32, final, 0, unroll=4)
        for t in range(tiles):
            copy = pltpu.make_async_copy(
                mm.at[t, pl.ds(8 + c * size, size), :],
                merged_out.at[pl.ds(c * size, size), pl.ds(t * LANES, LANES)],
                store_sem.at[c, t],
            )
            copy.start()
            stores.append(copy)
    for side in range(2):

        @pl.when(has[side])
        def _():
            strip_copy(side).wait_send()

    for n in range(SWEEPS + 1):
        all_z(n).wait_send()
    for k in range(SWEEPS):
        all_parts(k).wait_send()
        all_table(k).wait_send()
    for k in range(SWEEPS - 1):
        rows_sent(k + 2)
        for side in range(2):

            @pl.when(above[side])
            def _():
                extra_copy(k, side).wait_send()

            @pl.when(above[side] & enders[side])
            def _():
                all_halo_table(k, side).wait_send()

    for copy in stores:
        copy.wait()


def solution(mesh):
    zsize, along = mesh.shape["strip"], mesh.shape["along"]
    dims = (4, 4, 2) if along == 32 else (1, along // 2, 2)

    def on_device(heights, confidence, survey_ids, seam_mask, datum):
        rows, cols = heights.shape
        assert rows == 16 * along and cols % 256 == 0
        tiles = cols // LANES
        wide = (tiles + 1, rows, LANES)
        narrow = (tiles, rows, LANES)
        span = min(rows, LANES)
        strip = (rows // span, LANES, span)
        dma = pltpu.SemaphoreType.DMA
        scratch = [
            pltpu.VMEM((tiles + 1, rows + 16, LANES), F32),
            pltpu.VMEM(wide, I32),
            pltpu.VMEM(wide, F32),
            pltpu.VMEM(wide, F32),
            pltpu.VMEM(wide, F32),
            pltpu.VMEM(wide, F32),
            pltpu.VMEM(narrow, F32),
            pltpu.VMEM(wide, F32),
            pltpu.VMEM(wide, F32),
            pltpu.VMEM(narrow, I32),
            pltpu.VMEM((rows // 32, 256, cols), BF16),
            pltpu.VMEM((1, SURVEYS), F32),
            pltpu.VMEM((16, LANES), F32),
            pltpu.VMEM(strip, F32),
            pltpu.VMEM(strip, F32),
            pltpu.VMEM((SWEEPS, along, 8, LANES), F32),
            pltpu.VMEM((along, 2, 8, LANES), F32),
            pltpu.VMEM((SWEEPS, along, 8, LANES), F32),
            pltpu.VMEM((along, 2, 8, LANES), F32),
            pltpu.VMEM((HIGH, LANES), F32),
            pltpu.VMEM((SWEEPS + 1, 8, LANES), F32),
            pltpu.VMEM((SWEEPS + 1, zsize, 8, LANES), F32),
            pltpu.VMEM((SWEEPS, along, 8, LANES), F32),
            pltpu.VMEM((8, LANES), F32),
            pltpu.VMEM((SURVEYS, rows), F32),
            pltpu.VMEM((2, tiles + 1, 8, LANES), F32),
            pltpu.VMEM((2, tiles + 1, 8, LANES), I32),
            pltpu.VMEM((SWEEPS - 1, 2, tiles + 1, 8, LANES), F32),
            pltpu.VMEM((SWEEPS - 1, 2, tiles + 1, 8, LANES), F32),
            pltpu.VMEM((SWEEPS - 1, 2, 8, LANES), F32),
            pltpu.VMEM((SWEEPS - 1, 2, along, 8, LANES), F32),
            pltpu.VMEM((2, along, 2, 8, LANES), F32),
            pltpu.VMEM((HIGH, LANES), F32),
            dma((5, tiles)),
            dma((5, tiles)),
            dma((2,)),
            dma((2,)),
            dma((SWEEPS + 1, 2, 3)),
            dma((SWEEPS + 1, 2, 3)),
            dma((SWEEPS,)),
            dma((SWEEPS,)),
            dma((SWEEPS + 1,)),
            dma((SWEEPS + 1,)),
            dma((SWEEPS,)),
            dma((SWEEPS,)),
            dma((SWEEPS - 1, 2)),
            dma((SWEEPS - 1, 2)),
            dma((SWEEPS - 1, 2)),
            dma((SWEEPS - 1, 2)),
        ]
        return pl.pallas_call(
            functools.partial(kernel, zsize, dims),
            out_shape=(
                jax.ShapeDtypeStruct((rows, cols), F32),
                jax.ShapeDtypeStruct((SURVEYS, rows), F32),
            ),
            in_specs=[pl.BlockSpec(memory_space=pl.ANY)] * 5,
            out_specs=(pl.BlockSpec(memory_space=pl.ANY), pl.BlockSpec(memory_space=pl.ANY)),
            scratch_shapes=scratch,
            compiler_params=pltpu.CompilerParams(
                collective_id=0, has_side_effects=True, vmem_limit_bytes=52 * 1024 * 1024
            ),
        )(heights, confidence, survey_ids, seam_mask, datum.reshape(1, SURVEYS))

    return jax.shard_map(
        on_device,
        mesh=mesh,
        in_specs=(P("strip", "along"),) * 4 + (P(),),
        out_specs=(P("strip", "along"), P(None, "strip")),
        check_vma=False,
    )
```

```python
import functools

import jax
import jax.numpy as jnp
from jax import lax
from jax.experimental import pallas as pl
from jax.experimental.pallas import tpu as pltpu
from jax.sharding import PartitionSpec as P

SURVEYS = 40
SWEEPS = 4

smooth_weight = 1.0
centre_value = 1.05
half_width = 0.95

LANES = 128
HIGH = 5
DEPTH = 4
MESH = pl.DeviceIdType.MESH
F32 = jnp.float32
BF16 = jnp.bfloat16
I32 = jnp.int32


def coefficients():
    sigma_value = centre_value / half_width
    ratio_now = 1.0 / sigma_value
    pairs = [(0.0, 1.0 / centre_value)]
    for _ in range(SWEEPS - 1):
        ratio_next = 1.0 / (2.0 * sigma_value - ratio_now)
        pairs.append((ratio_next * ratio_now, 2.0 * ratio_next / half_width))
        ratio_now = ratio_next
    return pairs


def torus_distance(step, size):
    return min(step % size, (-step) % size)


def lane_take(values, index):
    return jnp.take_along_axis(values, index, axis=1, mode="promise_in_bounds")


def lanes_of(rows):
    return lax.broadcasted_iota(I32, (rows, LANES), 1)


def kernel(
    zsize,
    dims,
    heights,
    confidence,
    survey_ids,
    seam_mask,
    datum,
    merged_out,
    offsets_out,
    mm,
    ids,
    obs,
    q,
    cq,
    pp,
    w,
    d,
    bes,
    mask,
    onehot,
    datum_row,
    dat,
    strip_send,
    strip_recv,
    hist,
    hist_first,
    parts,
    parts_first,
    floor,
    zsend,
    zrecv,
    table,
    wtotal,
    offs,
    row_cq,
    row_ids,
    base_send,
    base_recv,
    halo_table,
    extra,
    extra_first,
    extra_floor,
    load_sem,
    store_sem,
    strip_ss,
    strip_rs,
    row_ss,
    row_rs,
    part_ss,
    part_rs,
    z_ss,
    z_rs,
    table_ss,
    table_rs,
    halo_ss,
    halo_rs,
    extra_ss,
    extra_rs,
):
    ny, nx, nc = dims
    along = ny * nx * nc
    rows, cols = heights.shape
    tiles = cols // LANES
    groups = rows // 32
    zi = lax.axis_index("strip")
    me = lax.axis_index("along")
    my_y, my_x, my_c = me // (nx * nc), (me // nc) % nx, me % nc

    steps = [(a, b, c) for a in range(ny) for b in range(nx) for c in range(nc)]
    steps = sorted(steps[1:], key=lambda s: -(torus_distance(s[0], ny) + torus_distance(s[1], nx) + 0.3 * s[2]))

    def turned(value, size):
        return [jnp.where(value + a >= size, value + a - size, value + a) for a in range(size)]

    ys, xs, cs = turned(my_y, ny), turned(my_x, nx), turned(my_c, nc)
    partners = {(a, b, c): (ys[a] * nx + xs[b]) * nc + cs[c] for a, b, c in [(0, 0, 0)] + steps}

    def partner(step):
        return partners[step]

    def slot_of(step):
        a, b, c = step
        return (((-a) % ny) * nx + (-b) % nx) * nc + (-c) % nc

    loads = {}
    load_order = [0, tiles - 1] + list(range(1, tiles - 1))
    def load(n, t):
        src, dst = ((survey_ids, ids), (confidence, cq), (heights, obs), (seam_mask, mask))[n]
        copy = pltpu.make_async_copy(src.at[:, pl.ds(t * LANES, LANES)], dst.at[t], load_sem.at[n, t])
        copy.start()
        loads[n, t] = copy

    for t in load_order:
        for n in range(3):
            load(n, t)

    datum_copy = pltpu.make_async_copy(datum, datum_row, load_sem.at[4, 0])
    datum_copy.start()

    mm[:, 0:8, :] = jnp.zeros((tiles + 1, 8, LANES), F32)
    mm[:, rows + 8 : rows + 16, :] = jnp.zeros((tiles + 1, 8, LANES), F32)
    strip_recv[...] = jnp.zeros(strip_recv.shape, F32)
    row_cq[...] = jnp.zeros(row_cq.shape, F32)
    row_ids[...] = jnp.zeros(row_ids.shape, I32)
    base_recv[...] = jnp.zeros(base_recv.shape, F32)
    halo_table[...] = jnp.zeros(halo_table.shape, F32)

    barrier = pltpu.get_barrier_semaphore()
    for step in steps:
        pl.semaphore_signal(barrier, inc=1, device_id=(zi, partner(step)), device_id_type=MESH)
    for k in range(1, zsize):
        pl.semaphore_signal(barrier, inc=1, device_id=((zi + k) % zsize, me), device_id_type=MESH)

    for side in range(2):
        inside = zi > 0 if side == 0 else zi < zsize - 1

        @pl.when(inside & (me == (0 if side == 0 else along - 1)))
        def _():
            for step in steps:
                to = (zi - 1 if side == 0 else zi + 1, partner(step))
                pl.semaphore_signal(barrier, inc=1, device_id=to, device_id_type=MESH)


    for t in range(tiles):
        load(3, t)
    for t in (0, tiles - 1):
        for n in range(3):
            loads[n, t].wait()
    datum_copy.wait()
    dat[...] = jnp.zeros((16, LANES), F32)
    dat[:, 0:SURVEYS] = jnp.broadcast_to(datum_row[...], (16, SURVEYS))

    def pack_strip(b, _):
        r = pl.ds(pl.multiple_of(b * 32, 32), 32)
        lane = lanes_of(32)
        first, last = 0, tiles - 1
        low = jnp.where(lane < 4, ids[first, r, :].astype(F32), pltpu.roll(cq[first, r, :], 4, 1))
        low = jnp.where(lane < 8, low, pltpu.roll(obs[first, r, :], 8, 1))
        high = jnp.where(lane >= 124, ids[last, r, :].astype(F32), pltpu.roll(cq[last, r, :], LANES - 4, 1))
        high = jnp.where(lane >= 120, high, pltpu.roll(obs[last, r, :], LANES - 8, 1))
        bes[0, r, :] = jnp.where(lane < 64, low, high)
        return 0

    lax.fori_loop(0, rows // 32, pack_strip, 0, unroll=4)
    span = min(rows, LANES)
    for b in range(rows // span):
        strip_send[b] = bes[0, b * span : (b + 1) * span, :].T

    greeted = jnp.where((zi > 0) & (me != along - 1), 1, 0) + jnp.where((zi < zsize - 1) & (me != 0), 1, 0)
    pl.semaphore_wait(barrier, along + zsize - 2 + greeted)


    def strip_copy(side):
        at = pl.ds(0, 16) if side == 0 else pl.ds(112, 16)
        return pltpu.make_async_remote_copy(
            strip_send.at[:, at, :],
            strip_recv.at[:, at, :],
            strip_ss.at[side],
            strip_rs.at[side],
            device_id=(zi, me - 1 if side == 0 else me + 1),
            device_id_type=MESH,
        )

    has = (me > 0, me < along - 1)
    for side in range(2):

        @pl.when(has[side])
        def _():
            strip_copy(side).start()

    def make_onehot(g):
        sub = lax.broadcasted_iota(I32, (8, LANES), 0)
        for t in range(tiles):
            block = ids[t, pl.ds(pl.multiple_of(g * 32, 32), 32), :] & 7
            for r in range(0, 32, 2):
                pair = [
                    jnp.where(jnp.broadcast_to(block[r + i : r + i + 1, :], (8, LANES)) == sub, 1.0, 0.0)
                    for i in range(2)
                ]
                onehot[g, r * 8 : r * 8 + 16, t * LANES : (t + 1) * LANES] = jnp.concatenate(pair, 0).astype(BF16)

    def profile(arrays, hid, g):
        pieces = []
        for values in arrays:
            high = values.astype(BF16)
            pieces += [high, (values - high.astype(F32)).astype(BF16)]
        zero = jnp.zeros_like(pieces[0])
        match = [hid == h for h in range(HIGH)]
        left = jnp.concatenate([jnp.where(m, p, zero) for p in pieces for m in match], 0)
        full = lax.dot_general(left, onehot[g], (((1,), (1,)), ((), ())), preferred_element_type=F32)
        lane = lanes_of(8)
        sub = lax.broadcasted_iota(I32, (8, LANES), 0)
        own_row = (lane >> 3) & 7
        out = []
        for n in range(len(arrays)):
            for j in range(2):
                tile = jnp.zeros((8, LANES), F32)
                for h in range(HIGH):
                    value = 0.0
                    for part in range(2):
                        at = ((2 * n + part) * HIGH + h) * 32 + 16 * j
                        pair = [full[at + 8 * i : at + 8 * i + 8, j * LANES : (j + 1) * LANES] for i in range(2)]
                        value += jnp.where(lane < 64, pair[0], pair[1])
                    value = jnp.take_along_axis(value, own_row, axis=0, mode="promise_in_bounds")
                    tile = jnp.where(sub == h, value, tile)
                out.append(tile)
        return out

    def high_bits(r):
        return jnp.concatenate([(ids[t, r, :] >> 3) & 7 for t in range(tiles)], 1)

    used = pl.ds(0, HIGH)

    def put_profile(k, g, sums):
        for j in range(2):
            if k == 0:
                hist_first[2 * g + j, 0] = sums[j]
                hist_first[2 * g + j, 1] = sums[2 + j]
            else:
                hist[k, 2 * g + j] = sums[j]

    def part_copy(k, to, slot):
        return pltpu.make_async_remote_copy(
            hist_first.at[to, :, used] if k == 0 else hist.at[k, to, used],
            parts_first.at[slot, :, used] if k == 0 else parts.at[k, slot, used],
            part_ss.at[k],
            part_rs.at[k],
            device_id=(zi, to),
            device_id_type=MESH,
        )

    def all_parts(k):
        many = pl.ds(1, along - 1)
        return pltpu.make_async_remote_copy(
            hist_first.at[many, :, used] if k == 0 else hist.at[k, many, used],
            parts_first.at[many, :, used] if k == 0 else parts.at[k, many, used],
            part_ss.at[k],
            part_rs.at[k],
            device_id=(zi, me),
            device_id_type=MESH,
        )

    def z_copy(n, k):
        return pltpu.make_async_remote_copy(
            zsend.at[n],
            zrecv.at[n, zsize - k],
            z_ss.at[n],
            z_rs.at[n],
            device_id=((zi + k) % zsize, me),
            device_id_type=MESH,
        )

    def all_z(n):
        return pltpu.make_async_remote_copy(
            zrecv.at[n, pl.ds(1, zsize - 1)],
            zrecv.at[n, pl.ds(1, zsize - 1)],
            z_ss.at[n],
            z_rs.at[n],
            device_id=(zi, me),
            device_id_type=MESH,
        )

    def send_total(n, total):
        zsend[n] = total
        zrecv[n, 0] = total
        for k in sorted(range(1, zsize), key=lambda k: -torus_distance(k, zsize)):
            z_copy(n, k).start()

    def send_inner(k):
        for step in steps:
            to = partner(step)

            @pl.when((to >= 2) & (to < along - 2))
            def _():
                part_copy(k, to, slot_of(step)).start()

    def send_outer(k):
        for to in (0, 1, along - 2, along - 1):
            y, x, c = to // (nx * nc), (to // nc) % nx, to % nc
            slot = (((my_y + ny - y) % ny) * nx + (my_x + nx - x) % nx) * nc + (my_c + nc - c) % nc

            @pl.when(me != to)
            def _():
                part_copy(k, to, slot).start()

        if k == 0:
            parts_first[0, :, 0:HIGH, :] = hist_first[me, :, 0:HIGH, :]
            send_total(0, jnp.sum(hist_first[:, 0], axis=0))
            send_total(SWEEPS, jnp.sum(hist_first[:, 1], axis=0))
        else:
            parts[k, 0, 0:HIGH, :] = hist[k, me, 0:HIGH, :]
            send_total(k, jnp.sum(hist[k], axis=0))

    def summed_z(n):
        all_z(n).wait_recv()
        return jnp.broadcast_to(jnp.sum(jnp.sum(zrecv[n], axis=0), keepdims=True), (8, LANES))

    above = (zi > 0, zi < zsize - 1)

    def row_copies(n, side):
        own, far = ((0, rows + 8), (rows - 8, 0))[side]
        own, far, shifted = pl.ds(own, 8), pl.ds(far, 8), pl.ds(own + 8, 8)
        every = pl.ds(0, tiles + 1)
        if n == 0:
            pairs = [(mm.at[pl.ds(0, tiles), shifted, :], mm.at[pl.ds(0, tiles), far, :])]
        elif n == 1:
            pairs = [
                (mm.at[pl.ds(tiles, 1), shifted, :], mm.at[pl.ds(tiles, 1), far, :]),
                (cq.at[every, own, :], row_cq.at[1 - side]),
                (ids.at[every, own, :], row_ids.at[1 - side]),
            ]
        else:
            pairs = [(base_send.at[n - 2, side], base_recv.at[n - 2, 1 - side])]
        return [
            pltpu.make_async_remote_copy(
                src,
                dst,
                row_ss.at[n, side, i],
                row_rs.at[n, side, i],
                device_id=(zi - 1 if side == 0 else zi + 1, me),
                device_id_type=MESH,
            )
            for i, (src, dst) in enumerate(pairs)
        ]

    def send_rows(n):
        for side in range(2):

            @pl.when(above[side])
            def _():
                for copy in row_copies(n, side):
                    copy.start()

    def wait_rows(n):
        for side in range(2):

            @pl.when(above[1 - side])
            def _():
                for copy in row_copies(n, side):
                    copy.wait_recv()

    def rows_sent(n):
        for side in range(2):

            @pl.when(above[side])
            def _():
                for copy in row_copies(n, side):
                    copy.wait_send()

    def prepare(g, t):
        r = pl.ds(pl.multiple_of(g * 32, 32), 32)
        upper = jnp.where(lax.broadcasted_iota(I32, (32, LANES), 0) & 8 > 0, 64, 0)
        survey = ids[t, r, :]
        weight = cq[t, r, :]
        seen = obs[t, r, :] + lane_take(jnp.concatenate([dat[...]] * 2, 0), survey)
        inverse = 1.0 / (weight + 4.0 * smooth_weight)
        if t == tiles:
            inside = weight > 0.0
            seen = jnp.where(inside, seen, 0.0)
            inverse = jnp.where(inside, inverse, 0.0)
        share = weight * inverse
        if t < tiles:
            w[t, r, :] = weight
        ids[t, r, :] = survey + upper
        obs[t, r, :] = seen
        q[t, r, :] = inverse
        cq[t, r, :] = share
        pp[t, r, :] = share * seen
        mm[t, pl.ds(pl.multiple_of(g * 32 + 8, 8), 32), :] = seen

    for t in load_order:

        def start_group(g, _, t=t):
            prepare(g, t)
            return 0

        for n in range(3):
            if t not in (0, tiles - 1):
                loads[n, t].wait()
        lax.fori_loop(0, groups, start_group, 0, unroll=8)
    send_rows(0)
    def own_onehot(g, _):
        make_onehot(g)
        return 0

    lax.fori_loop(0, groups, own_onehot, 0, unroll=8)
    for t in range(tiles):
        loads[3, t].wait()

    for side in range(2):

        @pl.when(has[1 - side])
        def _():
            strip_copy(side).wait_recv()

    def unpack_strip(g, _):
        r = pl.ds(pl.multiple_of(g * 32, 32), 32)
        lane = lanes_of(32)
        got = bes[0, r, :]
        edge_low, edge_high = lane < DEPTH, lane >= LANES - DEPTH
        ids[tiles, r, :] = jnp.where(edge_low | edge_high, got, 0.0).astype(I32)
        cq[tiles, r, :] = jnp.where(
            edge_low, pltpu.roll(got, LANES - 4, 1), jnp.where(edge_high, pltpu.roll(got, 4, 1), 0.0)
        )
        obs[tiles, r, :] = jnp.where(
            edge_low, pltpu.roll(got, LANES - 8, 1), jnp.where(edge_high, pltpu.roll(got, 8, 1), 0.0)
        )
        prepare(g, tiles)
        return 0

    blocks = rows // span
    order = [0, blocks - 1] + list(range(1, blocks - 1)) if blocks > 1 else [0]
    for i, b in enumerate(order):
        bes[0, b * span : (b + 1) * span, :] = strip_recv[b].T
        if i == min(1, blocks - 1):
            unpack_strip(0, 0)
            unpack_strip(groups - 1, 0)
            send_rows(1)
    lax.fori_loop(1, groups - 1, unpack_strip, 0, unroll=7)

    def stencil_group(k, g):
        first = g * 32
        r = pl.ds(pl.multiple_of(first, 32), 32)
        lane = lanes_of(32)
        now = [mm[t, pl.ds(pl.multiple_of(first + 8, 8), 32), :] for t in range(tiles + 1)]
        gaps, weights = [], []
        for t in range(tiles + 1):
            before, after = now[(t - 1) % (tiles + 1)], now[(t + 1) % (tiles + 1)]
            value = mm[t, pl.ds(first + 7, 32), :] + mm[t, pl.ds(first + 9, 32), :]
            value += pltpu.roll(jnp.where(lane == LANES - 1, before, now[t]), 1, 1)
            value += pltpu.roll(jnp.where(lane == 0, after, now[t]), LANES - 1, 1)
            bes[t, r, :] = value
            if t < tiles:
                if k == 0:
                    weight = mask[t, r, :].astype(F32) * w[t, r, :]
                    w[t, r, :] = weight
                    weights.append(weight)
                gaps.append(w[t, r, :] * (0.25 * value - obs[t, r, :]))
        arrays = [jnp.concatenate(gaps, 1)]
        if k == 0:
            arrays.append(jnp.concatenate(weights, 1))
        put_profile(k, g, profile(arrays, high_bits(r), g))

    def local_update(k, alpha, beta):
        def block(b, _):
            r = pl.ds(pl.multiple_of(b * 32, 32), 32)
            for t in range(tiles + 1):
                now = mm[t, pl.ds(pl.multiple_of(b * 32 + 8, 8), 32), :]
                value = beta * (pp[t, r, :] + q[t, r, :] * bes[t, r, :] - now)
                if k > 0:
                    value += alpha * d[t, r, :]
                d[t, r, :] = value
            return 0

        lax.fori_loop(0, rows // 32, block, 0, unroll=4)

    def row_tile(share):
        lane = lanes_of(8)
        sub = lax.broadcasted_iota(I32, (8, LANES), 0)
        index = 8 * (sub + jnp.where(lane >= 64, 8, 0)) + (lane & 7)
        kind = (lane & 63) >> 3
        tile = jnp.zeros((8, LANES), F32)
        for h in range(HIGH):
            tile = jnp.where(kind == h, lane_take(jnp.broadcast_to(share[h : h + 1], (8, LANES)), index), tile)
        return tile

    def owner_tile(k):
        gap_total = summed_z(k)
        if k == 0:
            weight_total = summed_z(SWEEPS)
            all_parts(0).wait_recv()
            floor[...] = 1.0 / jnp.maximum(jnp.sum(parts_first[:, 1, 0:HIGH, :], axis=0), 1.0)
            share = jnp.sum(parts_first[:, 0, 0:HIGH, :], axis=0) * floor[...]
        else:
            all_parts(k).wait_recv()
            share = jnp.sum(parts[k, :, 0:HIGH, :], axis=0) * floor[...]
        kind = (lanes_of(8) & 63) >> 3
        tile = row_tile(share)
        tile = jnp.where(kind == 5, gap_total, tile)
        if k == 0:
            tile = jnp.where(kind > 5, weight_total, tile)
        table[k, me] = tile

    def table_copy(k, step):
        return pltpu.make_async_remote_copy(
            table.at[k, me],
            table.at[k, me],
            table_ss.at[k],
            table_rs.at[k],
            device_id=(zi, partner(step)),
            device_id_type=MESH,
        )

    def all_table(k):
        return pltpu.make_async_remote_copy(
            table.at[k, pl.ds(0, along - 1)],
            table.at[k, pl.ds(0, along - 1)],
            table_ss.at[k],
            table_rs.at[k],
            device_id=(zi, me),
            device_id_type=MESH,
        )

    enders = (me == 0, me == along - 1)

    def extra_copy(k, side):
        tile = 0 if side == 0 else along - 1
        return pltpu.make_async_remote_copy(
            hist_first.at[tile, :, used] if k == 0 else hist.at[k, tile, used],
            extra_first.at[1 - side, me, :, used] if k == 0 else extra.at[k, 1 - side, me, used],
            extra_ss.at[k, side],
            extra_rs.at[k, 1 - side],
            device_id=(zi - 1 if side == 0 else zi + 1, along - 1 if side == 0 else 0),
            device_id_type=MESH,
        )

    def send_extra(k):
        for side in range(2):

            @pl.when(above[side])
            def _():
                extra_copy(k, side).start()

    def all_extra(k, side):
        return pltpu.make_async_remote_copy(
            hist_first.at[:, :, used] if k == 0 else hist.at[k, :, used],
            extra_first.at[side, :, :, used] if k == 0 else extra.at[k, side, :, used],
            extra_ss.at[k, side],
            extra_rs.at[k, side],
            device_id=(zi, me),
            device_id_type=MESH,
        )

    def halo_table_copy(k, side, step):
        return pltpu.make_async_remote_copy(
            halo_table.at[k, side],
            halo_table.at[k, side],
            halo_ss.at[k, side],
            halo_rs.at[k, side],
            device_id=(zi, partner(step)),
            device_id_type=MESH,
        )

    def all_halo_table(k, side):
        return pltpu.make_async_remote_copy(
            table.at[k, pl.ds(0, along - 1)],
            table.at[k, pl.ds(0, along - 1)],
            halo_ss.at[k, side],
            halo_rs.at[k, side],
            device_id=(zi, me),
            device_id_type=MESH,
        )

    def extra_tiles(k):
        for side in range(2):

            @pl.when(above[side] & enders[side])
            def _():
                all_extra(k, side).wait_recv()
                if k == 0:
                    total = jnp.sum(extra_first[side, :, 1, 0:HIGH, :], axis=0)
                    extra_floor[...] = 1.0 / jnp.maximum(total, 1.0)
                    share = jnp.sum(extra_first[side, :, 0, 0:HIGH, :], axis=0)
                else:
                    share = jnp.sum(extra[k, side, :, 0:HIGH, :], axis=0)
                halo_table[k, side] = row_tile(share * extra_floor[...])
                for step in steps:
                    halo_table_copy(k, side, step).start()

    def update_halo(k, beta, level):
        wait_rows(k + 2)
        for side in range(2):

            @pl.when(above[side])
            def _():
                @pl.when(jnp.logical_not(enders[side]))
                def _():
                    halo_table_copy(k, side, (0, 0, 0)).wait_recv()


            row_table = halo_table[k, side]
            at = (0, rows + 8)[side]
            for t in range(tiles + 1):
                step = beta * row_cq[side, t] * (lane_take(row_table, row_ids[side, t]) - level[:8])
                mm[t, at : at + 8, :] = base_recv[k, side, t] + step

    def update_group(g, beta, level, last):
        r = pl.ds(pl.multiple_of(g * 32, 32), 32)
        at = pl.ds(pl.multiple_of(g * 32 + 8, 8), 32)
        row_table = [table[last, 2 * g + i] for i in (0, 0, 1, 1)]
        row_table = jnp.concatenate(row_table, 0)
        for t in range(tiles if last == SWEEPS - 1 else tiles + 1):
            spread = lane_take(row_table, ids[t, r, :]) - level
            step = d[t, r, :] + beta * cq[t, r, :] * spread
            if last < SWEEPS - 1:
                d[t, r, :] = step
            mm[t, at, :] = mm[t, at, :] + step

    stores = []
    level, before = None, None
    for k, (alpha, beta) in enumerate(coefficients()):
        last = k == SWEEPS - 1
        if k == 0:

            def first(g, _):
                stencil_group(0, g)
                return 0

            lax.fori_loop(1, groups - 1, first, 0, unroll=14)
            send_inner(0)
            for n in range(2):
                wait_rows(n)
            for n in range(2):
                rows_sent(n)
        else:
            update_group(0, before, level, k - 1)
            update_group(1, before, level, k - 1)

            def both(g, _, k=k, before=before, level=level):
                update_group(g + 1, before, level, k - 1)
                stencil_group(k, g)
                return 0

            lax.fori_loop(1, groups - 1, both, 0, unroll=14)
            send_inner(k)
            update_halo(k - 1, before, level)
        stencil_group(k, 0)
        stencil_group(k, groups - 1)
        if not last:
            send_extra(k)
        send_outer(k)
        local_update(k, alpha, beta)
        if not last:
            for side, at in enumerate((0, rows - 8)):
                for t in range(tiles + 1):
                    base_send[k, side, t] = mm[t, at + 8 : at + 16, :] + d[t, at : at + 8, :]
            send_rows(k + 2)

        owner_tile(k)
        for step in steps:
            table_copy(k, step).start()
        if not last:
            extra_tiles(k)
        all_table(k).wait_recv()

        whole = jnp.sum(table[k], axis=0)
        if k == 0:
            wtotal[...] = 1.0 / (lane_take(whole, jnp.full((8, LANES), 48, I32)) + 1.0)
        level = lane_take(whole, jnp.full((8, LANES), 40, I32)) * wtotal[...]
        level = jnp.concatenate([level] * 4, 0)
        before = beta

    chunks = 2
    for b in range(rows // span):
        pieces = []
        for o in range(b * span // 16, (b + 1) * span // 16):
            piece = table[SWEEPS - 1, o] - level[:8]
            pieces += [piece, pltpu.roll(piece, 64, 1)]
        offs[:, b * span : (b + 1) * span] = jnp.concatenate(pieces, 0).T[:SURVEYS]
    copy = pltpu.make_async_copy(offs, offsets_out, store_sem.at[chunks, 0])
    copy.start()
    stores.append(copy)

    for c in range(chunks):
        size = rows // chunks

        def final(g, _, level=level):
            update_group(g, before, level, SWEEPS - 1)
            return 0

        lax.fori_loop(c * size // 32, (c + 1) * size // 32, final, 0, unroll=8)
        for t in range(tiles):
            copy = pltpu.make_async_copy(
                mm.at[t, pl.ds(8 + c * size, size), :],
                merged_out.at[pl.ds(c * size, size), pl.ds(t * LANES, LANES)],
                store_sem.at[c, t],
            )
            copy.start()
            stores.append(copy)
    for side in range(2):

        @pl.when(has[side])
        def _():
            strip_copy(side).wait_send()

    for n in range(SWEEPS + 1):
        all_z(n).wait_send()
    for k in range(SWEEPS):
        all_parts(k).wait_send()
        all_table(k).wait_send()
    for k in range(SWEEPS - 1):
        rows_sent(k + 2)
        for side in range(2):

            @pl.when(above[side])
            def _():
                extra_copy(k, side).wait_send()

            @pl.when(above[side] & enders[side])
            def _():
                all_halo_table(k, side).wait_send()

    for copy in stores:
        copy.wait()


def solution(mesh):
    zsize, along = mesh.shape["strip"], mesh.shape["along"]
    dims = (4, 4, 2) if along == 32 else (1, along // 2, 2)

    def on_device(heights, confidence, survey_ids, seam_mask, datum):
        rows, cols = heights.shape
        assert rows == 16 * along and cols % 256 == 0
        tiles = cols // LANES
        wide = (tiles + 1, rows, LANES)
        narrow = (tiles, rows, LANES)
        span = min(rows, LANES)
        strip = (rows // span, LANES, span)
        dma = pltpu.SemaphoreType.DMA
        scratch = [
            pltpu.VMEM((tiles + 1, rows + 16, LANES), F32),
            pltpu.VMEM(wide, I32),
            pltpu.VMEM(wide, F32),
            pltpu.VMEM(wide, F32),
            pltpu.VMEM(wide, F32),
            pltpu.VMEM(wide, F32),
            pltpu.VMEM(narrow, F32),
            pltpu.VMEM(wide, F32),
            pltpu.VMEM(wide, F32),
            pltpu.VMEM(narrow, I32),
            pltpu.VMEM((rows // 32, 256, cols), BF16),
            pltpu.VMEM((1, SURVEYS), F32),
            pltpu.VMEM((16, LANES), F32),
            pltpu.VMEM(strip, F32),
            pltpu.VMEM(strip, F32),
            pltpu.VMEM((SWEEPS, along, 8, LANES), F32),
            pltpu.VMEM((along, 2, 8, LANES), F32),
            pltpu.VMEM((SWEEPS, along, 8, LANES), F32),
            pltpu.VMEM((along, 2, 8, LANES), F32),
            pltpu.VMEM((HIGH, LANES), F32),
            pltpu.VMEM((SWEEPS + 1, 8, LANES), F32),
            pltpu.VMEM((SWEEPS + 1, zsize, 8, LANES), F32),
            pltpu.VMEM((SWEEPS, along, 8, LANES), F32),
            pltpu.VMEM((8, LANES), F32),
            pltpu.VMEM((SURVEYS, rows), F32),
            pltpu.VMEM((2, tiles + 1, 8, LANES), F32),
            pltpu.VMEM((2, tiles + 1, 8, LANES), I32),
            pltpu.VMEM((SWEEPS - 1, 2, tiles + 1, 8, LANES), F32),
            pltpu.VMEM((SWEEPS - 1, 2, tiles + 1, 8, LANES), F32),
            pltpu.VMEM((SWEEPS - 1, 2, 8, LANES), F32),
            pltpu.VMEM((SWEEPS - 1, 2, along, 8, LANES), F32),
            pltpu.VMEM((2, along, 2, 8, LANES), F32),
            pltpu.VMEM((HIGH, LANES), F32),
            dma((5, tiles)),
            dma((5, tiles)),
            dma((2,)),
            dma((2,)),
            dma((SWEEPS + 1, 2, 3)),
            dma((SWEEPS + 1, 2, 3)),
            dma((SWEEPS,)),
            dma((SWEEPS,)),
            dma((SWEEPS + 1,)),
            dma((SWEEPS + 1,)),
            dma((SWEEPS,)),
            dma((SWEEPS,)),
            dma((SWEEPS - 1, 2)),
            dma((SWEEPS - 1, 2)),
            dma((SWEEPS - 1, 2)),
            dma((SWEEPS - 1, 2)),
        ]
        return pl.pallas_call(
            functools.partial(kernel, zsize, dims),
            out_shape=(
                jax.ShapeDtypeStruct((rows, cols), F32),
                jax.ShapeDtypeStruct((SURVEYS, rows), F32),
            ),
            in_specs=[pl.BlockSpec(memory_space=pl.ANY)] * 5,
            out_specs=(pl.BlockSpec(memory_space=pl.ANY), pl.BlockSpec(memory_space=pl.ANY)),
            scratch_shapes=scratch,
            compiler_params=pltpu.CompilerParams(
                collective_id=0, has_side_effects=True, vmem_limit_bytes=52 * 1024 * 1024
            ),
        )(heights, confidence, survey_ids, seam_mask, datum.reshape(1, SURVEYS))

    return jax.shard_map(
        on_device,
        mesh=mesh,
        in_specs=(P("strip", "along"),) * 4 + (P(),),
        out_specs=(P("strip", "along"), P(None, "strip")),
        check_vma=False,
    )
```
